512 devices in a mesh: layer: 32 (over x_hi, y, core), lat: 16 (over x_lo, z).
Axes of the slice: x: 4 (x_hi: 2, x_lo: 2; x = x_hi * 2 + x_lo), y: 8, z: 8, core: 2. Of those that a mesh axis runs over, the one named last changes fastest.
Arguments:
- layer_inputs: bfloat16 [4, 3584, 704], P(None, 'lat', 'layer'), may hold values from -6 to 6
- layer_outputs: bfloat16 [704, 4, 3584], P('layer', None, 'lat'), may hold values from -6 to 6
- encoder: bfloat16 [4, 3584, 8192], P(None, 'lat', 'layer'), may hold values from -0.09375 to 0.09375
- encoder_bias: float32 [4, 8192], P(None, 'layer'), may hold values from -3 to 3
- decoder: bfloat16 [10, 3584, 8192], P(None, 'lat', 'layer'), may hold values from -0.1875 to 0.1875
- active_blocks: int32 [4, 22, 8], replicated, may hold values from 0 to 63, all different within a row; in each aligned block of 22 rows (0 to 21, 22 to 43, ..., all dimensions but the last counted through in order) at most 4 rows name the same one
Outputs:
- reconstruction: bfloat16 [704, 4, 3584], P('layer', None, 'lat')
- encoder_grad: bfloat16 [4, 3584, 8192], P(None, 'lat', 'layer')
- bias_grad: float32 [4, 8192], P(None, 'layer')
- decoder_grad: bfloat16 [10, 3584, 8192], P(None, 'lat', 'layer')
The draws below stay inside these ranges and needn't reach their ends.
Inputs may be any that keep to these rules, and one draw needn't show every extreme that they name: `active_blocks`: each list names 8 different latent blocks, and every block is named in some list. Among the 22 lists of one layer, no block is named by more than 4 lists, and in every draw some block of some layer is named by exactly 4.
All inputs are finite; a program needn't handle non-finite values.
Results may differ from the reference program's by a relative error of at most 0.0058.
Values may be sent and summed in bfloat16 or wider, within the bound.
A program may use at most 64 MiB of HBM per device.

```python
import math
import jax
import jax.numpy as jnp
import numpy as np

D = 3584
F = 8192
L = 4
BLOCK = 128
ROWBLOCK = 32
ACTIVE = 8
MOST = 4
ROWS = 704
NBLOCKS = 64
NROWBLOCKS = 22
PAIRS = 10


def block_scale(rng, extent, pieces, least, high):
    level = 1.0
    for axis_at, parts in pieces:
        draws = jax.random.uniform(jax.random.fold_in(jax.random.fold_in(rng, 6), axis_at), (parts,), jnp.float32, least / len(pieces), high / len(pieces))
        level = level * jnp.repeat(jnp.exp(draws), extent[axis_at] // parts).reshape((-1,) + (1,) * (len(extent) - 1 - axis_at))
    return level


def deal_out(stream_key, own, number, rows, amount, top, limit, lean):
    ranking = jax.random.permutation(stream_key, amount)
    crowded, ordinary = portions_of(amount, rows * top, limit, lean, True), portions_of(amount, rows * top, limit, lean, False)
    places = jnp.arange(amount)

    def named(sizes, offset_by):
        used = int((sizes > 0).sum())
        fixed = max(1, used // 4)
        passed = fixed + (places - fixed + offset_by * (used - fixed)) % max(1, amount - fixed)
        return jnp.zeros((amount,), jnp.int32).at[ranking[jnp.where(places < fixed, places, passed)]].set(jnp.asarray(sizes, jnp.int32))

    sizes = jnp.where(number % 4 == 0, named(crowded, number // 4), named(ordinary, number - number // 4 - 1))
    mixed = jax.random.permutation(jax.random.fold_in(own, 3), amount)
    source_of, taker = mixed[0:amount // 2 * 2:2], mixed[1:amount // 2 * 2:2]
    margin = jnp.minimum(sizes[source_of] - 1, limit - sizes[taker]) // 2
    margin = jnp.where((source_of == ranking[0]) | (taker == ranking[0]) | (sizes[taker] == 0), 0, jnp.maximum(margin, 0))
    passed = jax.random.randint(jax.random.fold_in(own, 4), (amount // 2,), 0, 1 << 20) % (margin + 1)
    sizes = sizes.at[source_of].add(-passed).at[taker].add(passed)
    items = jnp.searchsorted(jnp.cumsum(sizes), jnp.arange(rows * top), side="right").astype(jnp.int32)
    listing = items.reshape(top, rows).T
    listing = listing[jax.random.permutation(jax.random.fold_in(own, 1), rows)]
    offset_by = jax.random.randint(jax.random.fold_in(own, 2), (rows, 1), 0, top)
    return jnp.take_along_axis(listing, (jnp.arange(top)[None, :] + offset_by) % top, axis=1)


def portions_of(number_of, total, bound, slope, full):
    weights = [(1 << 20) // math.isqrt(grade ** slope) + 1 for grade in range(1, number_of + 1)]
    largest = bound if full else min(bound, max(-(-total // number_of), total * weights[0] // sum(weights)))
    least = 1 if total - largest >= number_of - 1 else 0
    holding, surplus = [largest] + [least] * (number_of - 1), total - largest - least * (number_of - 1)
    while surplus > 0:
        candidates = [i for i in range(1, number_of) if holding[i] < largest] or [i for i in range(1, number_of) if holding[i] < bound]
        pool, budget = sum([weights[i] for i in candidates]), surplus
        for i in candidates:
            more = min(bound - holding[i], max(1, budget * weights[i] // pool), surplus)
            holding[i] = holding[i] + more
            surplus = surplus - more
    return np.array(holding)


def scatter_about(rng, extent, scale, bound, shards=(), kind=jnp.bfloat16):
    result = scale * jax.random.normal(rng, extent, jnp.float32)
    if shards:
        result = result * block_scale(rng, extent, shards, -0.22, 0.18)
    return jnp.clip(result, -bound, bound).astype(kind)


def setup_inputs(seed: int = 0) -> dict:
    key_of = jax.random.split(jax.random.key(seed), 7)
    layer_inputs = scatter_about(key_of[0], (L, D, ROWS), 1.0, 6.0, ((1, 16), (2, 32)))
    layer_outputs = scatter_about(key_of[1], (ROWS, L, D), 1.0, 6.0, ((0, 32), (2, 16)))
    encoder = scatter_about(key_of[2], (L, D, F), D ** -0.5, 0.09375, ((1, 16), (2, 32)))
    encoder_bias = scatter_about(key_of[3], (L, F), 0.5, 3.0, ((1, 32),), jnp.float32)
    decoder = scatter_about(key_of[4], (PAIRS, D, F), (ACTIVE * BLOCK) ** -0.5, 0.1875, ((1, 16), (2, 32)))
    active_blocks_keys = jax.random.split(jax.random.fold_in(key_of[5], 1), L * NROWBLOCKS // NROWBLOCKS)
    active_blocks_turns = jax.random.permutation(jax.random.fold_in(key_of[5], 3), L * NROWBLOCKS // NROWBLOCKS)
    active_blocks = jax.vmap(lambda own, number: deal_out(jax.random.fold_in(key_of[5], 2), own, number, NROWBLOCKS, NBLOCKS, ACTIVE, MOST, 2))(active_blocks_keys, active_blocks_turns).reshape((L, NROWBLOCKS, ACTIVE))
    return dict(layer_inputs=layer_inputs, layer_outputs=layer_outputs, encoder=encoder, encoder_bias=encoder_bias, decoder=decoder, active_blocks=active_blocks)


def block_mask(active_blocks, lat_first, lat_count, row_total):
    onehot = jnp.any(active_blocks[:, :, :, None] == jnp.arange(NBLOCKS, dtype=jnp.int32)[None, None, None, :], axis=2)
    row_block = jnp.arange(row_total, dtype=jnp.int32) // ROWBLOCK
    lat_block = (lat_first + jnp.arange(lat_count, dtype=jnp.int32)) // BLOCK
    picked = jnp.take(onehot, row_block, axis=1)
    picked = jnp.take(picked, lat_block, axis=2)
    return jnp.transpose(picked, (0, 2, 1)).astype(jnp.float32)


def product(left, right):
    return jnp.dot(left.astype(jnp.float32), right.astype(jnp.float32), preferred_element_type=jnp.float32)


def reference(layer_inputs, layer_outputs, encoder, encoder_bias, decoder, active_blocks):
    pre_rows = []
    for source in range(L):
        pre_rows.append(product(encoder[source].T, layer_inputs[source]))
    pre_total = jnp.stack(pre_rows) + encoder_bias[:, :, None]
    live_mask = block_mask(active_blocks, 0, F, ROWS)
    latent_codes = (live_mask * jax.nn.softplus(pre_total)).astype(jnp.bfloat16)
    slope_vals = live_mask * jax.nn.sigmoid(pre_total)
    recon_rows = []
    for target in range(L):
        accum = jnp.zeros((D, ROWS), jnp.float32)
        for source in range(target + 1):
            pair_index = target * (target + 1) // 2 + source
            accum = accum + product(decoder[pair_index], latent_codes[source])
        recon_rows.append(accum.T)
    recon_full = jnp.stack(recon_rows, axis=1)
    error_all = (recon_full - layer_outputs.astype(jnp.float32)).astype(jnp.bfloat16)
    decoder_pieces = []
    for target in range(L):
        for source in range(target + 1):
            decoder_pieces.append(product(error_all[:, target, :].T, latent_codes[source].T).astype(jnp.bfloat16))
    decoder_grad = jnp.stack(decoder_pieces)
    grad_rows = []
    for source in range(L):
        accum = jnp.zeros((F, ROWS), jnp.float32)
        for target in range(source, L):
            pair_index = target * (target + 1) // 2 + source
            accum = accum + product(decoder[pair_index].T, error_all[:, target, :].T)
        grad_rows.append(accum)
    pre_grad = (jnp.stack(grad_rows) * slope_vals).astype(jnp.bfloat16)
    encoder_pieces = []
    for source in range(L):
        encoder_pieces.append(product(layer_inputs[source], pre_grad[source].T).astype(jnp.bfloat16))
    encoder_grad = jnp.stack(encoder_pieces)
    bias_grad = jnp.sum(pre_grad.astype(jnp.float32), axis=2)
    return recon_full.astype(jnp.bfloat16), encoder_grad, bias_grad, decoder_grad
```

```python
import functools

import jax
import jax.numpy as jnp
from jax import lax
from jax.experimental import pallas as pl
from jax.experimental.pallas import tpu as pltpu
from jax.sharding import PartitionSpec as P

BLOCK = 128
ROWBLOCK = 32
MOST = 4
SLOTS = MOST * ROWBLOCK
LANE = 128
BF, F32 = jnp.bfloat16, jnp.float32


def dot(a, b, dims=((1,), (0,))):
    return lax.dot_general(a, b, (dims, ((), ())), preferred_element_type=F32)


def iota(shape, dim):
    return lax.broadcasted_iota(jnp.int32, shape, dim)


def kernel(
    sizes,
    x_ref, y_ref, enc_ref, bias_ref, dec_ref, act_ref,
    rec_ref, eg_ref, bg_ref, dg_ref,
    xg, eg, xt, et, cd, pgd, encp, dcat, sel, selt,
    xy_s, xy_r, pk, rx, ck, pc, rc, pg, slope,
    hm_s, hm_r, ho, ra_s, ra_r, rb_s, rb_r, fx_s, fx_r, recb,
    load_sem, xy_sem, ag_x, ag_as, ag_ar, ag_bs, ag_br, ag_ms, ag_mr,
    lat_s, lat_r, hm_sem, rs_as, rs_ar, rs_bs, rs_br, fx_sem, rec_sem,
):
    layers, dl, lats, rows, ny, nl, chunk = sizes
    width = layers * dl
    span = 3 * LANE
    half = ny * chunk
    places = 2 * half
    real = 2 * rows
    shard = 2 * SLOTS // nl
    na, nb = ny // 2, ny // 2 - 1

    me, q = lax.axis_index("layer"), lax.axis_index("lat")
    core = lax.rem(me, 2)
    y = lax.rem(me // 2, ny)
    h = me // (2 * ny)
    owner = core == h
    step = 1 - 2 * core

    def at(hh, yy, cc):
        return {"layer": (hh * ny + yy) * 2 + cc, "lat": q}

    mate, partner = at(h, y, 1 - core), at(1 - h, y, core)
    y_a, y_b = lax.rem(y + step + ny, ny), lax.rem(y - step + ny, ny)
    to_a, to_b = at(h, y_a, core), at(h, y_b, core)

    def place(hh, offset):
        slot = lax.rem(y + step * offset + 2 * ny, ny)
        return pl.ds(pl.multiple_of((hh * ny + slot) * chunk, 16), chunk)

    def local(offset):
        return place(0, offset)

    barrier = pltpu.get_barrier_semaphore()
    for peer in (mate, partner, to_a, to_b):
        pl.semaphore_signal(barrier, inc=1, device_id=peer)

    def greet(d, carry):
        pl.semaphore_signal(barrier, inc=1, device_id={"layer": me, "lat": lax.rem(q + d, nl)})
        return carry

    lax.fori_loop(1, nl, greet, 0)
    pl.semaphore_wait(barrier, 4 + nl - 1)

    put = jnp.where(iota((chunk, rows), 0) == iota((chunk, rows), 1) + rows * core, 1.0, 0.0).astype(BF)
    xy_s[0:chunk, :] = dot(put, x_ref[...].reshape(width, rows), ((1,), (1,))).astype(BF)
    xy_s[chunk : 2 * chunk, :] = dot(put, y_ref[...]).astype(BF)
    xy_copy = pltpu.make_async_remote_copy(xy_s, xy_r, xy_sem.at[0], xy_sem.at[1], device_id=mate)
    xy_copy.start()

    encp[...] = jnp.zeros_like(encp)
    dcat[...] = jnp.zeros_like(dcat)
    loads = []

    def first(s):
        return min(dl * s // LANE * LANE, width - span)

    for s in range(layers):
        loads.append(pltpu.make_async_copy(enc_ref.at[s], encp.at[s, pl.ds(dl * s - first(s), dl)], load_sem.at[s]))
    for t in range(layers):
        for s in range(t + 1):
            pair = t * (t + 1) // 2 + s
            loads.append(
                pltpu.make_async_copy(
                    dec_ref.at[pair], dcat.at[pl.ds(dl * t, dl), pl.ds(lats * s, lats)], load_sem.at[layers + pair]
                )
            )
    for copy in loads:
        copy.start()

    xy_copy.wait_recv()
    xg_own = place(core, 0)

    def gather_copies(buf, n):
        def ring(to, offset, send, recv):
            where = buf.at[place(core, offset)]
            return pltpu.make_async_remote_copy(where, where, send, recv, device_id=to)

        cross = ring(partner, 0, ag_x.at[n, 0], ag_x.at[n, 1])
        a_out = [ring(to_a, -i, ag_as.at[n, i], ag_ar.at[n, i]) for i in range(na)]
        b_out = [ring(to_b, i, ag_bs.at[n, i], ag_br.at[n, i]) for i in range(nb)]
        a_in = [ring(to_a, -i - 1, ag_as.at[n, i], ag_ar.at[n, i]) for i in range(na)]
        b_in = [ring(to_b, i + 1, ag_bs.at[n, i], ag_br.at[n, i]) for i in range(nb)]
        order = [0]
        for i in range(na):
            order.append(-i - 1)
            if i < nb:
                order.append(i + 1)
        pass_on = [ring(mate, o, ag_ms.at[n, j], ag_mr.at[n, j]) for j, o in enumerate(order)]
        from_mate = []
        for j, o in enumerate(order):
            where = buf.at[place(1 - core, -o)]
            from_mate.append(pltpu.make_async_remote_copy(where, where, ag_ms.at[n, j], ag_mr.at[n, j], device_id=mate))
        return cross, a_out, b_out, a_in, b_in, pass_on, from_mate

    def gather_start(copies):
        cross, a_out, b_out, a_in, b_in, pass_on, from_mate = copies

        @pl.when(owner)
        def _():
            cross.start()

        @pl.when(jnp.logical_not(owner))
        def _():
            cross.wait_recv()

        a_out[0].start()
        if nb:
            b_out[0].start()
        pass_on[0].start()

    def gather_run(copies):
        cross, a_out, b_out, a_in, b_in, pass_on, from_mate = copies
        j = 1
        for i in range(na):
            a_in[i].wait_recv()
            if i + 1 < na:
                a_out[i + 1].start()
            pass_on[j].start()
            j += 1
            if i < nb:
                b_in[i].wait_recv()
                if i + 1 < nb:
                    b_out[i + 1].start()
                pass_on[j].start()
                j += 1
        for copy in from_mate:
            copy.wait_recv()

    def gather_end(copies):
        cross, a_out, b_out, a_in, b_in, pass_on, from_mate = copies

        @pl.when(owner)
        def _():
            cross.wait_send()

        for copy in a_out + b_out + pass_on:
            copy.wait_send()

    x_copies = gather_copies(xg, 0)

    @pl.when(owner)
    def _():
        xg[xg_own, :] = xy_s[0:chunk, :] + xy_r[0:chunk, :]

    gather_start(x_copies)

    nr = act_ref.shape[1]
    ii, jj = iota((nr, nr), 0), iota((nr, nr), 1)
    lane_place = iota((1, places), 1)
    lane_chip = jnp.zeros((1, places), jnp.int32)
    for c in range(1, 2 * ny):
        lane_chip = lane_chip + jnp.where(lane_place >= c * chunk, 1, 0)
    lane_in = lane_place - lane_chip * chunk
    lane_row = jnp.where(lane_in < real, lane_chip * real + lane_in, -2).astype(F32)
    m0, r1 = iota((SLOTS, nr), 0), iota((SLOTS, nr), 1)
    r0, m1 = iota((nr, SLOTS), 0), iota((nr, SLOTS), 1)
    col_rank = (m0 // ROWBLOCK).astype(F32)
    col_value = (ROWBLOCK * r1 + m0 % ROWBLOCK + 1).astype(F32)
    row_rank = (m1 // ROWBLOCK).astype(F32)
    row_value = (ROWBLOCK * r0 + m1 % ROWBLOCK + 1).astype(F32)
    chip_in = iota((chunk, SLOTS), 0)

    def choose(s, carry):
        named = act_ref[s]
        for b in range(2):
            hit = jnp.max(jnp.where(named == 2 * me + b, 1.0, 0.0), axis=1, keepdims=True)
            across = jnp.broadcast_to(hit, (nr, nr))
            hit_row = jnp.sum(jnp.where(ii == jj, across, 0.0), axis=0, keepdims=True)
            rank_row = jnp.sum(jnp.where(ii < jj, across, 0.0), axis=0, keepdims=True)
            rank = jnp.sum(jnp.where(jj < ii, jnp.broadcast_to(hit_row, (nr, nr)), 0.0), axis=1, keepdims=True)
            rank_row = jnp.where(hit_row > 0, rank_row, -1.0)
            rank = jnp.where(hit > 0, rank, -1.0)
            want = jnp.sum(jnp.where(rank_row == col_rank, col_value, 0.0), axis=1, keepdims=True) - 1.0
            want_row = jnp.sum(jnp.where(rank == row_rank, row_value, 0.0), axis=0, keepdims=True) - 1.0
            sel[s, b * SLOTS : (b + 1) * SLOTS, :] = jnp.where(want == lane_row, 1.0, 0.0).astype(BF)
            for c in range(2 * ny):
                row = jnp.where(chip_in < real, chip_in + c * real, -2).astype(F32)
                selt[s, c * chunk : (c + 1) * chunk, b * SLOTS : (b + 1) * SLOTS] = jnp.where(
                    row == want_row, 1.0, 0.0
                ).astype(BF)
        return carry

    lax.fori_loop(0, layers, choose, 0)

    gather_run(x_copies)
    for copy in loads[:layers]:
        copy.wait()

    def lat_rows(j):
        return pl.ds(pl.multiple_of(j * shard, 16), shard)

    def scatter(src, dst, s, n):
        def one(d, carry):
            peer = lax.rem(q + d, nl)
            pltpu.make_async_remote_copy(
                src.at[s, lat_rows(peer)], dst.at[s, q], lat_s.at[n, s], lat_r.at[n, s],
                device_id={"layer": me, "lat": peer},
            ).start()
            return carry

        lax.fori_loop(1, nl, one, 0)
        dst[s, q] = src[s, lat_rows(q), :]

    def spread(buf, s, n):
        def one(d, carry):
            where = buf.at[s, lat_rows(q)]
            pltpu.make_async_remote_copy(
                where, where, lat_s.at[n, s], lat_r.at[n, s], device_id={"layer": me, "lat": lax.rem(q + d, nl)}
            ).start()
            return carry

        lax.fori_loop(1, nl, one, 0)

    def lat_wait(sem, s, n):
        where = ck.at[s, pl.ds(0, (nl - 1) * shard)]
        pltpu.make_async_copy(where, where, sem.at[n, s]).wait()

    def pack(dense, dst, s):
        both = dot(sel[s], dense)
        for b in range(2):
            part = slice(b * SLOTS, (b + 1) * SLOTS)
            dst[s, part, :] = both[part, b * BLOCK : (b + 1) * BLOCK].astype(BF)

    for s in range(layers):
        dense = dot(xg[:, first(s) : first(s) + span], encp[s]).astype(BF)
        pack(dense, pk, s)
        scatter(pk, rx, s, 0)

    for n in range(width // LANE):
        xt[n * LANE : (n + 1) * LANE, :] = xg[:, n * LANE : (n + 1) * LANE].T

    b_of = q * shard // SLOTS
    for s in range(layers):
        lat_wait(lat_r, s, 0)
        total = jnp.sum(rx[s].astype(F32), axis=0)
        bias = jnp.where(b_of == 0, bias_ref[s : s + 1, 0:BLOCK], bias_ref[s : s + 1, BLOCK : 2 * BLOCK])
        pre = total + bias
        small = jnp.exp(-jnp.abs(pre))
        ck[s, lat_rows(q), :] = (jnp.maximum(pre, 0.0) + jnp.log1p(small)).astype(BF)
        slope[s] = jnp.where(pre >= 0, 1.0, small) / (1.0 + small)
        spread(ck, s, 1)

    def unpack(src, dst, s):
        zero = jnp.zeros((SLOTS, BLOCK), BF)
        wide = jnp.concatenate(
            [
                jnp.concatenate([src[s, 0:SLOTS, :], zero], axis=1),
                jnp.concatenate([zero, src[s, SLOTS : 2 * SLOTS, :]], axis=1),
            ],
            axis=0,
        )
        dst[:, s * lats : (s + 1) * lats] = dot(selt[s], wide).astype(BF)

    for s in range(layers):
        lat_wait(lat_r, s, 1)
        unpack(ck, cd, s)

    for copy in loads[layers:]:
        copy.wait()

    tiles = [min(layers, ((n + 1) * LANE - 1) // dl + 1) for n in range(width // LANE)]
    groups = []
    for n, count in enumerate(tiles):
        if groups and groups[-1][2] == count:
            groups[-1][1] = n + 1
        else:
            groups.append([n, n + 1, count])

    def decode(hh, out):
        base = pl.ds(pl.multiple_of(hh * half, 16), half)
        for lo, hi, count in groups:
            lanes = slice(lo * LANE, hi * LANE)
            out[:, lanes] = dot(cd[base, 0 : count * lats], dcat[lanes, 0 : count * lats], ((1,), (1,))).astype(out.dtype)

    decode(1 - core, hm_s)
    hm_copy = pltpu.make_async_remote_copy(hm_s, hm_r, hm_sem.at[0], hm_sem.at[1], device_id=mate)
    hm_copy.start()
    decode(core, ho)
    hm_copy.wait_recv()

    def mine(offset):
        return ho[local(offset), :] + hm_r[local(offset), :].astype(F32)

    a_copies = [
        pltpu.make_async_remote_copy(ra_s.at[i], ra_r.at[i], rs_as.at[i], rs_ar.at[i], device_id=to_a) for i in range(na)
    ]
    b_copies = [
        pltpu.make_async_remote_copy(rb_s.at[i], rb_r.at[i], rs_bs.at[i], rs_br.at[i], device_id=to_b) for i in range(nb)
    ]
    for i in range(na):
        part = mine(na - i)
        if i:
            a_copies[i - 1].wait_recv()
            part = part + ra_r[i - 1].astype(F32)
        ra_s[i] = part.astype(BF)
        a_copies[i].start()
        if i < nb:
            part = mine(i - nb)
            if i:
                b_copies[i - 1].wait_recv()
                part = part + rb_r[i - 1].astype(F32)
            rb_s[i] = part.astype(BF)
            b_copies[i].start()
    total = mine(0)
    a_copies[na - 1].wait_recv()
    total = total + ra_r[na - 1].astype(F32)
    if nb:
        b_copies[nb - 1].wait_recv()
        total = total + rb_r[nb - 1].astype(F32)
    ho[local(0), :] = total

    fx_copy = pltpu.make_async_remote_copy(fx_s, fx_r, fx_sem.at[0], fx_sem.at[1], device_id=partner)
    rec_copy = pltpu.make_async_remote_copy(recb, recb, rec_sem.at[0], rec_sem.at[1], device_id=mate)
    e_copies = gather_copies(eg, 1)

    @pl.when(jnp.logical_not(owner))
    def _():
        fx_s[...] = ho[local(0), :].astype(BF)
        fx_copy.start()

    @pl.when(owner)
    def _():
        fx_copy.wait_recv()
        whole = ho[local(0), :] + fx_r[...].astype(F32)
        outs = xy_s[chunk : 2 * chunk, :].astype(F32) + xy_r[chunk : 2 * chunk, :].astype(F32)
        eg[xg_own, :] = (whole - outs).astype(BF)
        recb[...] = whole.astype(BF)

    gather_start(e_copies)

    @pl.when(owner)
    def _():
        rec_copy.start()

    gather_run(e_copies)

    for s in range(layers - 1, -1, -1):
        low = dl * s // LANE * LANE
        dense = dot(eg[:, low:width], dcat[low:width, s * lats : (s + 1) * lats]).astype(BF)
        pack(dense, pc, s)
        scatter(pc, rc, s, 2)

    for n in range(width // LANE):
        et[n * LANE : (n + 1) * LANE, :] = eg[:, n * LANE : (n + 1) * LANE].T

    def decoder_grad(t):
        out = dot(et[t * dl : (t + 1) * dl, :], cd[:, 0 : (t + 1) * lats])
        for s in range(t + 1):
            dg_ref[t * (t + 1) // 2 + s] = out[:, s * lats : (s + 1) * lats].astype(BF)

    decoder_grad(0)
    decoder_grad(1)

    for s in range(layers - 1, -1, -1):
        lat_wait(lat_r, s, 2)
        total = jnp.sum(rc[s].astype(F32), axis=0)
        pg[s, lat_rows(q), :] = (total * slope[s]).astype(BF)
        spread(pg, s, 3)

    decoder_grad(2)
    decoder_grad(3)

    for s in range(layers - 1, -1, -1):
        lat_wait(lat_r, s, 3)
        unpack(pg, pgd, s)
        for b in range(2):
            bg_ref[s : s + 1, b * BLOCK : (b + 1) * BLOCK] = jnp.sum(
                pg[s, b * SLOTS : (b + 1) * SLOTS, :].astype(F32), axis=0, keepdims=True
            )
        eg_ref[s] = dot(xt[s * dl : (s + 1) * dl, :], pgd[:, s * lats : (s + 1) * lats]).astype(BF)

    @pl.when(owner)
    def _():
        rec_copy.wait_send()

    @pl.when(jnp.logical_not(owner))
    def _():
        fx_copy.wait_send()
        rec_copy.wait_recv()

    take = jnp.where(iota((rows, chunk), 1) == iota((rows, chunk), 0) + rows * core, 1.0, 0.0).astype(BF)
    rec_ref[...] = dot(take, recb[...]).astype(BF)

    xy_copy.wait_send()
    hm_copy.wait_send()
    for copy in a_copies + b_copies:
        copy.wait_send()
    gather_end(x_copies)
    gather_end(e_copies)
    for n in range(4):
        for s in range(layers):
            lat_wait(lat_s, s, n)


def step(sizes, layer_inputs, layer_outputs, encoder, encoder_bias, decoder, active_blocks):
    layers, dl, lats, rows, ny, nl, chunk = sizes
    width = layers * dl
    places = 2 * ny * chunk
    na, nb = ny // 2, max(1, ny // 2 - 1)
    shard = 2 * SLOTS // nl
    pairs = decoder.shape[0]
    vmem, dma = pltpu.VMEM, pltpu.SemaphoreType.DMA
    ring = (chunk, width)
    scratch = [
        vmem((places, width), BF),
        vmem((places, width), BF),
        vmem((width, places), BF),
        vmem((width, places), BF),
        vmem((places, layers * lats), BF),
        vmem((places, layers * lats), BF),
        vmem((layers, 3 * LANE, lats), BF),
        vmem((width, layers * lats), BF),
        vmem((layers, 2 * SLOTS, places), BF),
        vmem((layers, places, 2 * SLOTS), BF),
        vmem((2 * chunk, width), BF),
        vmem((2 * chunk, width), BF),
        vmem((layers, 2 * SLOTS, BLOCK), BF),
        vmem((layers, nl, shard, BLOCK), BF),
        vmem((layers, 2 * SLOTS, BLOCK), BF),
        vmem((layers, 2 * SLOTS, BLOCK), BF),
        vmem((layers, nl, shard, BLOCK), BF),
        vmem((layers, 2 * SLOTS, BLOCK), BF),
        vmem((layers, shard, BLOCK), F32),
        vmem((places // 2, width), BF),
        vmem((places // 2, width), BF),
        vmem((places // 2, width), F32),
        vmem((na,) + ring, BF),
        vmem((na,) + ring, BF),
        vmem((nb,) + ring, BF),
        vmem((nb,) + ring, BF),
        vmem(ring, BF),
        vmem(ring, BF),
        vmem(ring, BF),
        dma((layers + pairs,)),
        dma((2,)),
        dma((2, 2)),
        dma((2, na)),
        dma((2, na)),
        dma((2, nb)),
        dma((2, nb)),
        dma((2, ny)),
        dma((2, ny)),
        dma((4, layers)),
        dma((4, layers)),
        dma((2,)),
        dma((na,)),
        dma((na,)),
        dma((nb,)),
        dma((nb,)),
        dma((2,)),
        dma((2,)),
    ]
    in_vmem = pl.BlockSpec(memory_space=pltpu.VMEM)
    anywhere = pl.BlockSpec(memory_space=pl.ANY)
    rec, eg, bg, dg = pl.pallas_call(
        functools.partial(kernel, sizes),
        out_shape=(
            jax.ShapeDtypeStruct((rows, width), BF),
            jax.ShapeDtypeStruct((layers, dl, lats), BF),
            jax.ShapeDtypeStruct((layers, lats), F32),
            jax.ShapeDtypeStruct((pairs, dl, lats), BF),
        ),
        in_specs=[in_vmem, in_vmem, anywhere, in_vmem, anywhere, in_vmem],
        out_specs=(in_vmem,) * 4,
        scratch_shapes=scratch,
        compiler_params=pltpu.CompilerParams(
            collective_id=0, has_side_effects=True, vmem_limit_bytes=48 * 1024 * 1024
        ),
    )(layer_inputs, layer_outputs.reshape(rows, width), encoder, encoder_bias, decoder, active_blocks)
    return rec.reshape(rows, layers, dl), eg, bg, dg


def solution(mesh):
    ny, nl = mesh.shape["layer"] // 4, mesh.shape["lat"]

    def local(layer_inputs, layer_outputs, encoder, encoder_bias, decoder, active_blocks):
        layers, dl, lats = encoder.shape
        rows = layer_outputs.shape[0]
        chunk = -(-2 * rows // 16) * 16
        sizes = (layers, dl, lats, rows, ny, nl, chunk)
        return step(sizes, layer_inputs, layer_outputs, encoder, encoder_bias, decoder, active_blocks)

    return jax.shard_map(
        local,
        mesh=mesh,
        in_specs=(
            P(None, "lat", "layer"),
            P("layer", None, "lat"),
            P(None, "lat", "layer"),
            P(None, "layer"),
            P(None, "lat", "layer"),
            P(),
        ),
        out_specs=(
            P("layer", None, "lat"),
            P(None, "lat", "layer"),
            P(None, "layer"),
            P(None, "lat", "layer"),
        ),
        check_vma=False,
    )
```

```python
import functools

import jax
import jax.numpy as jnp
from jax import lax
from jax.experimental import pallas as pl
from jax.experimental.pallas import tpu as pltpu
from jax.sharding import PartitionSpec as P

BLOCK = 128
ROWBLOCK = 32
MOST = 4
SLOTS = MOST * ROWBLOCK
LANE = 128
BF, F32 = jnp.bfloat16, jnp.float32


def dot(a, b, dims=((1,), (0,))):
    return lax.dot_general(a, b, (dims, ((), ())), preferred_element_type=F32)


def iota(shape, dim):
    return lax.broadcasted_iota(jnp.int32, shape, dim)


def kernel(
    sizes,
    x_ref, y_ref, enc_ref, bias_ref, dec_ref, act_ref,
    rec_ref, eg_ref, bg_ref, dg_ref,
    xg, eg, xt, et, cd, pgd, encp, dcat, sel, selt,
    xy_s, xy_r, pk, rx, ck, pc, rc, pg, slope,
    hm_s, hm_r, ho, ra_s, ra_r, rb_s, rb_r, fx_s, fx_r, recb, yc, x_in, y_in, act_in, bias_in,
    load_sem, xy_out, xy_sem, ag_as, ag_ar, ag_bs, ag_br, ag_ms, ag_mr,
    lat_s, lat_r, hm_sem, rs_as, rs_ar, rs_bs, rs_br, fx_sem, rec_sem,
):
    layers, dl, lats, rows, ny, nl, chunk = sizes
    width = layers * dl
    span = 3 * LANE
    half = ny * chunk
    places = 2 * half
    real = 2 * rows
    shard = 2 * SLOTS // nl
    na, nb = ny // 2, ny // 2 - 1

    me, q = lax.axis_index("layer"), lax.axis_index("lat")
    core = lax.rem(me, 2)
    y = lax.rem(me // 2, ny)
    h = me // (2 * ny)
    owner = core == h
    step = 1 - 2 * core

    def at(hh, yy, cc):
        return {"layer": (hh * ny + yy) * 2 + cc, "lat": q}

    mate, partner = at(h, y, 1 - core), at(1 - h, y, core)
    y_a, y_b = lax.rem(y + step + ny, ny), lax.rem(y - step + ny, ny)
    to_a, to_b = at(h, y_a, core), at(h, y_b, core)

    def place(hh, offset):
        slot = lax.rem(y + step * offset + 2 * ny, ny)
        return pl.ds(pl.multiple_of((hh * ny + slot) * chunk, 16), chunk)

    def local(offset):
        return place(0, offset)

    diagonal = at(1 - h, y, 1 - core)

    barrier = pltpu.get_barrier_semaphore()
    for peer in (mate, partner, diagonal, to_a, to_b):
        pl.semaphore_signal(barrier, inc=1, device_id=peer)

    def greet(d, carry):
        pl.semaphore_signal(barrier, inc=1, device_id={"layer": me, "lat": lax.rem(q + d, nl)})
        return carry

    lax.fori_loop(1, nl, greet, 0)

    loads = [
        pltpu.make_async_copy(x_ref, x_in, load_sem.at[0]),
        pltpu.make_async_copy(y_ref, y_in, load_sem.at[1]),
        pltpu.make_async_copy(act_ref, act_in, load_sem.at[2]),
        pltpu.make_async_copy(bias_ref, bias_in, load_sem.at[3]),
    ]
    for copy in loads:
        copy.start()
    encp[...] = jnp.zeros_like(encp)
    dcat[...] = jnp.zeros_like(dcat)

    def first(s):
        return min(dl * s // LANE * LANE, width - span)

    enc_loads, dec_loads = [], []
    for s in range(layers):
        where = encp.at[s, pl.ds(dl * s - first(s), dl)]
        enc_loads.append(pltpu.make_async_copy(enc_ref.at[s], where, load_sem.at[4 + s]))
    for t in range(layers):
        for s in range(t + 1):
            pair = t * (t + 1) // 2 + s
            where = dcat.at[pl.ds(dl * t, dl), pl.ds(lats * s, lats)]
            dec_loads.append(pltpu.make_async_copy(dec_ref.at[pair], where, load_sem.at[4 + layers + pair]))
    for copy in enc_loads + dec_loads:
        copy.start()

    def flat(ref):
        return jnp.concatenate([ref[:, s, :] for s in range(layers)], axis=1)

    pad = jnp.zeros((32 - rows, width), BF)
    loads[0].wait()
    xy_s[0] = jnp.concatenate([flat(x_in), pad], axis=0)
    loads[1].wait()
    xy_s[1] = jnp.concatenate([flat(y_in), pad], axis=0)

    pl.semaphore_wait(barrier, 5 + nl - 1)

    def xy_copy(n, to, w):
        return pltpu.make_async_remote_copy(
            xy_s.at[n], xy_r.at[n, w], xy_out.at[n, w], xy_sem.at[n, w], device_id=to
        )

    for n in range(2):
        @pl.when(owner)
        def _():
            xy_copy(n, partner, core).start()

        @pl.when(jnp.logical_not(owner))
        def _():
            xy_copy(n, mate, core).start()
            pltpu.make_async_remote_copy(
                xy_s.at[n], xy_r.at[n, core], xy_out.at[n, 1 - core], xy_sem.at[n, core], device_id=diagonal
            ).start()

    def merged(n):
        total = None
        for w in range(2):
            there, here = iota((chunk, 32), 0), iota((chunk, 32), 1)
            put = jnp.where((there == here + rows * w) & (here < rows), 1.0, 0.0).astype(BF)
            part = dot(put, xy_r[n, w])
            total = part if total is None else total + part
        return total.astype(BF)

    def xy_arrive(n):
        @pl.when(owner)
        def _():
            xy_r[n, core] = xy_s[n]
            xy_copy(n, mate, 1 - core).wait_recv()

        @pl.when(jnp.logical_not(owner))
        def _():
            for w in range(2):
                xy_copy(n, mate, w).wait_recv()

        return merged(n)

    cuts = [(0, 3 * LANE), (3 * LANE, 5 * LANE), (5 * LANE, width)]
    nc = len(cuts)

    def gather_copies(buf, n):
        def ring(to, offset, send, recv, lanes):
            where = buf.at[place(core, offset), pl.ds(lanes[0], lanes[1] - lanes[0])]
            return pltpu.make_async_remote_copy(where, where, send, recv, device_id=to)

        def rings(to, sign, shift, count, send, recv):
            return [
                [ring(to, sign * (i + shift), send.at[n, i, c], recv.at[n, i, c], cuts[c]) for c in range(nc)]
                for i in range(count)
            ]

        a_out, a_in = rings(to_a, -1, 0, na, ag_as, ag_ar), rings(to_a, -1, 1, na, ag_as, ag_ar)
        b_out, b_in = rings(to_b, 1, 0, nb, ag_bs, ag_br), rings(to_b, 1, 1, nb, ag_bs, ag_br)
        order = [0]
        for i in range(na):
            order.append(-i - 1)
            if i < nb:
                order.append(i + 1)
        pass_on, from_mate = [], []
        for j, o in enumerate(order):
            where = buf.at[place(core, o)]
            pass_on.append(
                pltpu.make_async_remote_copy(where, where, ag_ms.at[n, j], ag_mr.at[n, j], device_id=mate)
            )
            where = buf.at[place(1 - core, -o)]
            from_mate.append(
                pltpu.make_async_remote_copy(where, where, ag_ms.at[n, j], ag_mr.at[n, j], device_id=mate)
            )
        return a_out, b_out, a_in, b_in, pass_on, from_mate

    def gather_start(copies, c):
        copies[0][0][c].start()
        if nb:
            copies[1][0][c].start()

    def gather_run(copies, extra):
        a_out, b_out, a_in, b_in, pass_on, from_mate = copies
        pass_on[0].start()
        j = 1
        for i in range(na):
            for c in range(nc):
                a_in[i][c].wait_recv()
                if i + 1 < na:
                    a_out[i + 1][c].start()
                if i < nb:
                    b_in[i][c].wait_recv()
                    if i + 1 < nb:
                        b_out[i + 1][c].start()
            for _ in range(2 if i < nb else 1):
                pass_on[j].start()
                j += 1
            if i < len(extra):
                extra[i]()
        for more in extra[na:]:
            more()
        for copy in from_mate:
            copy.wait_recv()

    def gather_end(copies):
        a_out, b_out, a_in, b_in, pass_on, from_mate = copies
        for group in a_out + b_out:
            for copy in group:
                copy.wait_send()
        for copy in pass_on:
            copy.wait_send()

    own = place(core, 0)
    x_copies = gather_copies(xg, 0)
    xg[own, :] = xy_arrive(0)
    for c in range(nc):
        gather_start(x_copies, c)

    nr = act_in.shape[2]
    ii, jj = iota((nr, nr), 0), iota((nr, nr), 1)
    lane_place = iota((1, places), 1)
    lane_chip = jnp.zeros((1, places), jnp.int32)
    for c in range(1, 2 * ny):
        lane_chip = lane_chip + jnp.where(lane_place >= c * chunk, 1, 0)
    lane_in = lane_place - lane_chip * chunk
    lane_row = jnp.where(lane_in < real, lane_chip * real + lane_in, -2).astype(F32)
    m0, r1 = iota((SLOTS, nr), 0), iota((SLOTS, nr), 1)
    r0, m1 = iota((nr, SLOTS), 0), iota((nr, SLOTS), 1)
    col_rank = (m0 // ROWBLOCK).astype(F32)
    col_value = (ROWBLOCK * r1 + m0 % ROWBLOCK + 1).astype(F32)
    row_rank = (m1 // ROWBLOCK).astype(F32)
    row_value = (ROWBLOCK * r0 + m1 % ROWBLOCK + 1).astype(F32)
    chip_in = iota((chunk, SLOTS), 0)
    chip_row = jnp.where(chip_in < real, chip_in, -places).astype(F32)
    loads[2].wait()
    loads[3].wait()

    def choose(s):
        named = act_in[s]
        for b in range(2):
            hit_row = jnp.max(jnp.where(named == 2 * me + b, 1.0, 0.0), axis=0, keepdims=True)
            across = jnp.broadcast_to(hit_row, (nr, nr))
            hit = jnp.sum(jnp.where(ii == jj, across, 0.0), axis=1, keepdims=True)
            rank = jnp.sum(jnp.where(jj < ii, across, 0.0), axis=1, keepdims=True)
            rank_row = jnp.sum(jnp.where(ii < jj, jnp.broadcast_to(hit, (nr, nr)), 0.0), axis=0, keepdims=True)
            rank_row = jnp.where(hit_row > 0, rank_row, -1.0)
            rank = jnp.where(hit > 0, rank, -1.0)
            want = jnp.sum(jnp.where(rank_row == col_rank, col_value, 0.0), axis=1, keepdims=True) - 1.0
            want_row = jnp.sum(jnp.where(rank == row_rank, row_value, 0.0), axis=0, keepdims=True) - 1.0
            sel[s, b * SLOTS : (b + 1) * SLOTS, :] = jnp.where(want == lane_row, 1.0, 0.0).astype(BF)
            for c in range(2 * ny):
                selt[s, c * chunk : (c + 1) * chunk, b * SLOTS : (b + 1) * SLOTS] = jnp.where(
                    chip_row == want_row - float(c * real), 1.0, 0.0
                ).astype(BF)

    def outputs():
        yc[...] = xy_arrive(1)

    choose(0)
    gather_run(x_copies, [functools.partial(choose, s) for s in range(1, layers)] + [outputs])
    for copy in enc_loads:
        copy.wait()

    def lat_rows(j):
        return pl.ds(pl.multiple_of(j * shard, 16), shard)

    def scatter(src, dst, s, n):
        def one(d, carry):
            peer = lax.rem(q + d, nl)
            pltpu.make_async_remote_copy(
                src.at[s, lat_rows(peer)], dst.at[s, q], lat_s.at[n, s], lat_r.at[n, s],
                device_id={"layer": me, "lat": peer},
            ).start()
            return carry

        lax.fori_loop(1, nl, one, 0)
        dst[s, q] = src[s, lat_rows(q), :]

    def spread(buf, s, n):
        def one(d, carry):
            where = buf.at[s, lat_rows(q)]
            pltpu.make_async_remote_copy(
                where, where, lat_s.at[n, s], lat_r.at[n, s], device_id={"layer": me, "lat": lax.rem(q + d, nl)}
            ).start()
            return carry

        lax.fori_loop(1, nl, one, 0)

    def lat_wait(sem, s, n):
        where = ck.at[s, pl.ds(0, (nl - 1) * shard)]
        pltpu.make_async_copy(where, where, sem.at[n, s]).wait()

    def pack(dense, dst, s):
        both = dot(sel[s], dense)
        for b in range(2):
            part = slice(b * SLOTS, (b + 1) * SLOTS)
            dst[s, part, :] = both[part, b * BLOCK : (b + 1) * BLOCK].astype(BF)

    for s in range(layers):
        dense = dot(xg[:, first(s) : first(s) + span], encp[s]).astype(BF)
        pack(dense, pk, s)
        scatter(pk, rx, s, 0)

    for n in range(width // LANE):
        xt[n * LANE : (n + 1) * LANE, :] = xg[:, n * LANE : (n + 1) * LANE].T

    b_of = q * shard // SLOTS
    for s in range(layers):
        lat_wait(lat_r, s, 0)
        total = jnp.sum(rx[s].astype(F32), axis=0)
        bias = jnp.where(b_of == 0, bias_in[s : s + 1, 0:BLOCK], bias_in[s : s + 1, BLOCK : 2 * BLOCK])
        pre = total + bias
        small = jnp.exp(-jnp.abs(pre))
        ck[s, lat_rows(q), :] = (jnp.maximum(pre, 0.0) + jnp.log1p(small)).astype(BF)
        slope[s] = jnp.where(pre >= 0, 1.0, small) / (1.0 + small)
        spread(ck, s, 1)

    def unpack(src, dst, s):
        zero = jnp.zeros((SLOTS, BLOCK), BF)
        wide = jnp.concatenate(
            [
                jnp.concatenate([src[s, 0:SLOTS, :], zero], axis=1),
                jnp.concatenate([zero, src[s, SLOTS : 2 * SLOTS, :]], axis=1),
            ],
            axis=0,
        )
        dst[:, s * lats : (s + 1) * lats] = dot(selt[s], wide).astype(BF)

    for s in range(layers):
        lat_wait(lat_r, s, 1)
        unpack(ck, cd, s)

    for copy in dec_loads:
        copy.wait()

    tiles = [min(layers, ((n + 1) * LANE - 1) // dl + 1) for n in range(width // LANE)]
    groups = []
    for n, count in enumerate(tiles):
        if groups and groups[-1][2] == count:
            groups[-1][1] = n + 1
        else:
            groups.append([n, n + 1, count])

    def decode(hh, out, c):
        base = pl.ds(pl.multiple_of(hh * half, 16), half)
        for lo, hi, count in groups:
            if cuts[c][0] <= lo * LANE < cuts[c][1]:
                lanes = slice(lo * LANE, hi * LANE)
                part = dot(cd[base, 0 : count * lats], dcat[lanes, 0 : count * lats], ((1,), (1,)))
                out[:, lanes] = part.astype(out.dtype)

    def lanes_of(c):
        return pl.ds(cuts[c][0], cuts[c][1] - cuts[c][0])

    hm_copies = []
    for c in range(nc):
        decode(1 - core, hm_s, c)
        hm_copies.append(
            pltpu.make_async_remote_copy(
                hm_s.at[:, lanes_of(c)], hm_r.at[:, lanes_of(c)], hm_sem.at[0, c], hm_sem.at[1, c], device_id=mate
            )
        )
        hm_copies[c].start()

    def mine(offset, c):
        return ho[local(offset), lanes_of(c)] + hm_r[local(offset), lanes_of(c)].astype(F32)

    def sums(to, count, buf_s, buf_r, send, recv):
        return [
            [
                pltpu.make_async_remote_copy(
                    buf_s.at[i, :, lanes_of(c)], buf_r.at[i, :, lanes_of(c)], send.at[i, c], recv.at[i, c], device_id=to
                )
                for c in range(nc)
            ]
            for i in range(count)
        ]

    a_copies = sums(to_a, na, ra_s, ra_r, rs_as, rs_ar)
    b_copies = sums(to_b, nb, rb_s, rb_r, rs_bs, rs_br)

    def forward(copies, buf_s, buf_r, i, offset, c):
        part = mine(offset, c)
        if i:
            copies[i - 1][c].wait_recv()
            part = part + buf_r[i - 1, :, lanes_of(c)].astype(F32)
        buf_s[i, :, lanes_of(c)] = part.astype(BF)
        copies[i][c].start()

    for i in range(na):
        for c in range(nc):
            if i == 0:
                decode(core, ho, c)
                hm_copies[c].wait_recv()
            forward(a_copies, ra_s, ra_r, i, na - i, c)
            if i < nb:
                forward(b_copies, rb_s, rb_r, i, i - nb, c)
    fx_copies = []
    for c in range(nc):
        total = mine(0, c)
        a_copies[na - 1][c].wait_recv()
        total = total + ra_r[na - 1, :, lanes_of(c)].astype(F32)
        if nb:
            b_copies[nb - 1][c].wait_recv()
            total = total + rb_r[nb - 1, :, lanes_of(c)].astype(F32)
        fx_s[:, lanes_of(c)] = total.astype(BF)
        fx_copies.append(
            pltpu.make_async_remote_copy(
                fx_s.at[:, lanes_of(c)], fx_r.at[:, lanes_of(c)], fx_sem.at[0, c], fx_sem.at[1, c], device_id=partner
            )
        )
        fx_copies[c].start()

    e_copies = gather_copies(eg, 1)
    for c in range(nc):
        fx_copies[c].wait_recv()
        lanes = lanes_of(c)
        whole = fx_s[:, lanes].astype(F32) + fx_r[:, lanes].astype(F32)
        eg[own, lanes] = (whole - yc[:, lanes].astype(F32)).astype(BF)
        gather_start(e_copies, c)

        @pl.when(owner)
        def _():
            recb[:, lanes] = whole.astype(BF)

    rec_copy = pltpu.make_async_remote_copy(recb, recb, rec_sem.at[0], rec_sem.at[1], device_id=mate)

    @pl.when(owner)
    def _():
        rec_copy.start()

    gather_run(e_copies, [])

    for s in range(layers - 1, -1, -1):
        low = dl * s // LANE * LANE
        dense = dot(eg[:, low:width], dcat[low:width, s * lats : (s + 1) * lats]).astype(BF)
        pack(dense, pc, s)
        scatter(pc, rc, s, 2)

    for n in range(width // LANE):
        et[n * LANE : (n + 1) * LANE, :] = eg[:, n * LANE : (n + 1) * LANE].T

    def decoder_grad(t):
        out = dot(et[t * dl : (t + 1) * dl, :], cd[:, 0 : (t + 1) * lats])
        for s in range(t + 1):
            dg_ref[t * (t + 1) // 2 + s] = out[:, s * lats : (s + 1) * lats].astype(BF)

    decoder_grad(0)
    decoder_grad(1)

    for s in range(layers - 1, -1, -1):
        lat_wait(lat_r, s, 2)
        total = jnp.sum(rc[s].astype(F32), axis=0)
        pg[s, lat_rows(q), :] = (total * slope[s]).astype(BF)
        spread(pg, s, 3)

    decoder_grad(2)
    decoder_grad(3)

    for s in range(layers - 1, -1, -1):
        lat_wait(lat_r, s, 3)
        unpack(pg, pgd, s)
        for b in range(2):
            bg_ref[s : s + 1, b * BLOCK : (b + 1) * BLOCK] = jnp.sum(
                pg[s, b * SLOTS : (b + 1) * SLOTS, :].astype(F32), axis=0, keepdims=True
            )
        eg_ref[s] = dot(xt[s * dl : (s + 1) * dl, :], pgd[:, s * lats : (s + 1) * lats]).astype(BF)

    @pl.when(owner)
    def _():
        rec_copy.wait_send()

    @pl.when(jnp.logical_not(owner))
    def _():
        rec_copy.wait_recv()

    take = jnp.where(iota((rows, chunk), 1) == iota((rows, chunk), 0) + rows * core, 1.0, 0.0).astype(BF)
    rec_ref[...] = dot(take, recb[...]).astype(BF)

    for n in range(2):
        xy_copy(n, mate, core).wait_send()

        @pl.when(jnp.logical_not(owner))
        def _():
            xy_copy(n, mate, 1 - core).wait_send()

    for copy in hm_copies + fx_copies:
        copy.wait_send()
    for group in a_copies + b_copies:
        for copy in group:
            copy.wait_send()
    gather_end(x_copies)
    gather_end(e_copies)
    for n in range(4):
        for s in range(layers):
            lat_wait(lat_s, s, n)


def step(sizes, layer_inputs, layer_outputs, encoder, encoder_bias, decoder, active_blocks):
    layers, dl, lats, rows, ny, nl, chunk = sizes
    width = layers * dl
    places = 2 * ny * chunk
    na, nb = ny // 2, max(1, ny // 2 - 1)
    shard = 2 * SLOTS // nl
    pairs = decoder.shape[0]
    vmem, dma = pltpu.VMEM, pltpu.SemaphoreType.DMA
    ring = (chunk, width)
    scratch = [
        vmem((places, width), BF),
        vmem((places, width), BF),
        vmem((width, places), BF),
        vmem((width, places), BF),
        vmem((places, layers * lats), BF),
        vmem((places, layers * lats), BF),
        vmem((layers, 3 * LANE, lats), BF),
        vmem((width, layers * lats), BF),
        vmem((layers, 2 * SLOTS, places), BF),
        vmem((layers, places, 2 * SLOTS), BF),
        vmem((2, 32, width), BF),
        vmem((2, 2, 32, width), BF),
        vmem((layers, 2 * SLOTS, BLOCK), BF),
        vmem((layers, nl, shard, BLOCK), BF),
        vmem((layers, 2 * SLOTS, BLOCK), BF),
        vmem((layers, 2 * SLOTS, BLOCK), BF),
        vmem((layers, nl, shard, BLOCK), BF),
        vmem((layers, 2 * SLOTS, BLOCK), BF),
        vmem((layers, shard, BLOCK), F32),
        vmem((places // 2, width), BF),
        vmem((places // 2, width), BF),
        vmem((places // 2, width), F32),
        vmem((na,) + ring, BF),
        vmem((na,) + ring, BF),
        vmem((nb,) + ring, BF),
        vmem((nb,) + ring, BF),
        vmem(ring, BF),
        vmem(ring, BF),
        vmem(ring, BF),
        vmem(ring, BF),
        vmem((rows, layers, dl), BF),
        vmem((rows, layers, dl), BF),
        vmem((layers, active_blocks.shape[2], active_blocks.shape[1]), jnp.int32),
        vmem((layers, lats), F32),
        dma((4 + layers + pairs,)),
        dma((2, 2)),
        dma((2, 2)),
        dma((2, na, 3)),
        dma((2, na, 3)),
        dma((2, nb, 3)),
        dma((2, nb, 3)),
        dma((2, ny)),
        dma((2, ny)),
        dma((4, layers)),
        dma((4, layers)),
        dma((2, 3)),
        dma((na, 3)),
        dma((na, 3)),
        dma((nb, 3)),
        dma((nb, 3)),
        dma((2, 3)),
        dma((2,)),
    ]
    in_vmem = pl.BlockSpec(memory_space=pltpu.VMEM)
    anywhere = pl.BlockSpec(memory_space=pl.ANY)
    rec, eg, bg, dg = pl.pallas_call(
        functools.partial(kernel, sizes),
        out_shape=(
            jax.ShapeDtypeStruct((rows, width), BF),
            jax.ShapeDtypeStruct((layers, dl, lats), BF),
            jax.ShapeDtypeStruct((layers, lats), F32),
            jax.ShapeDtypeStruct((pairs, dl, lats), BF),
        ),
        in_specs=[anywhere] * 6,
        out_specs=(in_vmem,) * 4,
        scratch_shapes=scratch,
        compiler_params=pltpu.CompilerParams(
            collective_id=0, has_side_effects=True, vmem_limit_bytes=60 * 1024 * 1024
        ),
    )(
        layer_inputs.transpose(2, 0, 1),
        layer_outputs,
        encoder,
        encoder_bias,
        decoder,
        active_blocks.transpose(0, 2, 1),
    )
    return rec.reshape(rows, layers, dl), eg, bg, dg


def solution(mesh):
    ny, nl = mesh.shape["layer"] // 4, mesh.shape["lat"]

    def local(layer_inputs, layer_outputs, encoder, encoder_bias, decoder, active_blocks):
        layers, dl, lats = encoder.shape
        rows = layer_outputs.shape[0]
        chunk = -(-2 * rows // 16) * 16
        sizes = (layers, dl, lats, rows, ny, nl, chunk)
        return step(sizes, layer_inputs, layer_outputs, encoder, encoder_bias, decoder, active_blocks)

    return jax.shard_map(
        local,
        mesh=mesh,
        in_specs=(
            P(None, "lat", "layer"),
            P("layer", None, "lat"),
            P(None, "lat", "layer"),
            P(None, "layer"),
            P(None, "lat", "layer"),
            P(),
        ),
        out_specs=(
            P("layer", None, "lat"),
            P(None, "lat", "layer"),
            P(None, "layer"),
            P(None, "lat", "layer"),
        ),
        check_vma=False,
    )
```

```python
import functools

import jax
import jax.numpy as jnp
from jax import lax
from jax.experimental import pallas as pl
from jax.experimental.pallas import tpu as pltpu
from jax.sharding import PartitionSpec as P

BLOCK = 128
ROWBLOCK = 32
MOST = 4
SLOTS = MOST * ROWBLOCK
LANE = 128
BF, F32 = jnp.bfloat16, jnp.float32


def dot(a, b, dims=((1,), (0,))):
    return lax.dot_general(a, b, (dims, ((), ())), preferred_element_type=F32)


def iota(shape, dim):
    return lax.broadcasted_iota(jnp.int32, shape, dim)


def kernel(
    sizes,
    x_ref, y_ref, enc_ref, bias_ref, dec_ref, act_ref,
    rec_ref, eg_ref, bg_ref, dg_ref,
    xg, eg, xt, et, cd, pgd, encp, dcat, sel, selt,
    xy_s, xy_r, xs, xr, keep, zs, zr, cz, slope,
    hm_s, hm_r, ho, ra_s, ra_r, rb_s, rb_r, fx_s, fx_r, recb, yc, x_in, y_in, act_in, bias_in,
    load_sem, xy_out, xy_sem, ag_as, ag_ar, ag_bs, ag_br, ag_ms, ag_mr,
    x_out, x_arr, z_out, z_arr, c_out, c_arr, cx_out, cx_arr, hm_sem, rs_as, rs_ar, rs_bs, rs_br, fx_sem, rec_sem,
):
    layers, dl, lats, rows, ny, nl, chunk = sizes
    width = layers * dl
    span = 3 * LANE
    half = ny * chunk
    places = 2 * half
    real = 2 * rows
    nz = nl // 2
    shard = SLOTS // nz
    na, nb = ny // 2, ny // 2 - 1

    me, q = lax.axis_index("layer"), lax.axis_index("lat")
    core = lax.rem(me, 2)
    y = lax.rem(me // 2, ny)
    h = me // (2 * ny)
    owner = core == h
    step = 1 - 2 * core

    def at(hh, yy, cc):
        return {"layer": (hh * ny + yy) * 2 + cc, "lat": q}

    mate, partner = at(h, y, 1 - core), at(1 - h, y, core)
    y_a, y_b = lax.rem(y + step + ny, ny), lax.rem(y - step + ny, ny)
    to_a, to_b = at(h, y_a, core), at(h, y_b, core)

    def place(hh, offset):
        slot = lax.rem(y + step * offset + 2 * ny, ny)
        return pl.ds(pl.multiple_of((hh * ny + slot) * chunk, 16), chunk)

    def local(offset):
        return place(0, offset)

    diagonal = at(1 - h, y, 1 - core)
    x_lo, z = q // nz, lax.rem(q, nz)
    beside = {"layer": me, "lat": (1 - x_lo) * nz + z}

    def along(d):
        return {"layer": me, "lat": x_lo * nz + lax.rem(z + d, nz)}

    barrier = pltpu.get_barrier_semaphore()
    for peer in (mate, partner, diagonal, to_a, to_b, beside):
        pl.semaphore_signal(barrier, inc=1, device_id=peer)

    def greet(d, carry):
        pl.semaphore_signal(barrier, inc=1, device_id=along(d))
        return carry

    lax.fori_loop(1, nz, greet, 0)

    loads = [
        pltpu.make_async_copy(x_ref, x_in, load_sem.at[0]),
        pltpu.make_async_copy(y_ref, y_in, load_sem.at[1]),
        pltpu.make_async_copy(act_ref, act_in, load_sem.at[2]),
        pltpu.make_async_copy(bias_ref, bias_in, load_sem.at[3]),
    ]
    for copy in loads:
        copy.start()
    encp[...] = jnp.zeros_like(encp)
    dcat[...] = jnp.zeros_like(dcat)

    def first(s):
        return min(dl * s // LANE * LANE, width - span)

    enc_loads, dec_loads = [], []
    for s in range(layers):
        where = encp.at[s, pl.ds(dl * s - first(s), dl)]
        enc_loads.append(pltpu.make_async_copy(enc_ref.at[s], where, load_sem.at[4 + s]))
    for t in range(layers):
        for s in range(t + 1):
            pair = t * (t + 1) // 2 + s
            where = dcat.at[pl.ds(dl * t, dl), pl.ds(lats * s, lats)]
            dec_loads.append(pltpu.make_async_copy(dec_ref.at[pair], where, load_sem.at[4 + layers + pair]))
    for copy in enc_loads + dec_loads:
        copy.start()

    def flat(ref):
        return jnp.concatenate([ref[:, s, :] for s in range(layers)], axis=1)

    pad = jnp.zeros((32 - rows, width), BF)
    loads[0].wait()
    xy_s[0] = jnp.concatenate([flat(x_in), pad], axis=0)
    loads[1].wait()
    xy_s[1] = jnp.concatenate([flat(y_in), pad], axis=0)

    pl.semaphore_wait(barrier, 6 + nz - 1)

    def xy_copy(n, to, w):
        return pltpu.make_async_remote_copy(
            xy_s.at[n], xy_r.at[n, w], xy_out.at[n, w], xy_sem.at[n, w], device_id=to
        )

    for n in range(2):
        @pl.when(owner)
        def _():
            xy_copy(n, partner, core).start()

        @pl.when(jnp.logical_not(owner))
        def _():
            xy_copy(n, mate, core).start()
            pltpu.make_async_remote_copy(
                xy_s.at[n], xy_r.at[n, core], xy_out.at[n, 1 - core], xy_sem.at[n, core], device_id=diagonal
            ).start()

    def merged(n):
        total = None
        for w in range(2):
            there, here = iota((chunk, 32), 0), iota((chunk, 32), 1)
            put = jnp.where((there == here + rows * w) & (here < rows), 1.0, 0.0).astype(BF)
            part = dot(put, xy_r[n, w])
            total = part if total is None else total + part
        return total.astype(BF)

    def xy_arrive(n):
        @pl.when(owner)
        def _():
            xy_r[n, core] = xy_s[n]
            xy_copy(n, mate, 1 - core).wait_recv()

        @pl.when(jnp.logical_not(owner))
        def _():
            for w in range(2):
                xy_copy(n, mate, w).wait_recv()

        return merged(n)

    cuts = [(0, 3 * LANE), (3 * LANE, 5 * LANE), (5 * LANE, width)]
    nc = len(cuts)

    def gather_copies(buf, n):
        def ring(to, offset, send, recv, lanes):
            where = buf.at[place(core, offset), pl.ds(lanes[0], lanes[1] - lanes[0])]
            return pltpu.make_async_remote_copy(where, where, send, recv, device_id=to)

        def rings(to, sign, shift, count, send, recv):
            return [
                [ring(to, sign * (i + shift), send.at[n, i, c], recv.at[n, i, c], cuts[c]) for c in range(nc)]
                for i in range(count)
            ]

        a_out, a_in = rings(to_a, -1, 0, na, ag_as, ag_ar), rings(to_a, -1, 1, na, ag_as, ag_ar)
        b_out, b_in = rings(to_b, 1, 0, nb, ag_bs, ag_br), rings(to_b, 1, 1, nb, ag_bs, ag_br)
        order = [0]
        for i in range(na):
            order.append(-i - 1)
            if i < nb:
                order.append(i + 1)
        pass_on, from_mate = [], []
        for j, o in enumerate(order):
            where = buf.at[place(core, o)]
            pass_on.append(
                pltpu.make_async_remote_copy(where, where, ag_ms.at[n, j], ag_mr.at[n, j], device_id=mate)
            )
            where = buf.at[place(1 - core, -o)]
            from_mate.append(
                pltpu.make_async_remote_copy(where, where, ag_ms.at[n, j], ag_mr.at[n, j], device_id=mate)
            )
        return a_out, b_out, a_in, b_in, pass_on, from_mate

    def gather_start(copies, c):
        copies[0][0][c].start()
        if nb:
            copies[1][0][c].start()

    def gather_run(copies, extra):
        a_out, b_out, a_in, b_in, pass_on, from_mate = copies
        pass_on[0].start()
        j = 1
        for i in range(na):
            for c in range(nc):
                a_in[i][c].wait_recv()
                if i + 1 < na:
                    a_out[i + 1][c].start()
                if i < nb:
                    b_in[i][c].wait_recv()
                    if i + 1 < nb:
                        b_out[i + 1][c].start()
            for _ in range(2 if i < nb else 1):
                pass_on[j].start()
                j += 1
            if i < len(extra):
                extra[i]()
        for more in extra[na:]:
            more()
        for copy in from_mate:
            copy.wait_recv()

    def gather_end(copies):
        a_out, b_out, a_in, b_in, pass_on, from_mate = copies
        for group in a_out + b_out:
            for copy in group:
                copy.wait_send()
        for copy in pass_on:
            copy.wait_send()

    own = place(core, 0)
    x_copies = gather_copies(xg, 0)
    xg[own, :] = xy_arrive(0)
    for c in range(nc):
        gather_start(x_copies, c)

    nr = act_in.shape[2]
    ii, jj = iota((nr, nr), 0), iota((nr, nr), 1)
    lane_place = iota((1, places), 1)
    lane_chip = jnp.zeros((1, places), jnp.int32)
    for c in range(1, 2 * ny):
        lane_chip = lane_chip + jnp.where(lane_place >= c * chunk, 1, 0)
    lane_in = lane_place - lane_chip * chunk
    lane_row = jnp.where(lane_in < real, lane_chip * real + lane_in, -2).astype(F32)
    m0, r1 = iota((SLOTS, nr), 0), iota((SLOTS, nr), 1)
    r0, m1 = iota((nr, SLOTS), 0), iota((nr, SLOTS), 1)
    col_rank = (m0 // ROWBLOCK).astype(F32)
    col_value = (ROWBLOCK * r1 + m0 % ROWBLOCK + 1).astype(F32)
    row_rank = (m1 // ROWBLOCK).astype(F32)
    row_value = (ROWBLOCK * r0 + m1 % ROWBLOCK + 1).astype(F32)
    chip_in = iota((chunk, SLOTS), 0)
    chip_row = jnp.where(chip_in < real, chip_in, -places).astype(F32)
    loads[2].wait()
    loads[3].wait()

    def choose(s):
        named = act_in[s]
        for b in range(2):
            hit_row = jnp.max(jnp.where(named == 2 * me + b, 1.0, 0.0), axis=0, keepdims=True)
            across = jnp.broadcast_to(hit_row, (nr, nr))
            hit = jnp.sum(jnp.where(ii == jj, across, 0.0), axis=1, keepdims=True)
            rank = jnp.sum(jnp.where(jj < ii, across, 0.0), axis=1, keepdims=True)
            rank_row = jnp.sum(jnp.where(ii < jj, jnp.broadcast_to(hit, (nr, nr)), 0.0), axis=0, keepdims=True)
            rank_row = jnp.where(hit_row > 0, rank_row, -1.0)
            rank = jnp.where(hit > 0, rank, -1.0)
            want = jnp.sum(jnp.where(rank_row == col_rank, col_value, 0.0), axis=1, keepdims=True) - 1.0
            want_row = jnp.sum(jnp.where(rank == row_rank, row_value, 0.0), axis=0, keepdims=True) - 1.0
            sel[s, b * SLOTS : (b + 1) * SLOTS, :] = jnp.where(want == lane_row, 1.0, 0.0).astype(BF)
            for c in range(2 * ny):
                selt[s, c * chunk : (c + 1) * chunk, b * SLOTS : (b + 1) * SLOTS] = jnp.where(
                    chip_row == want_row - float(c * real), 1.0, 0.0
                ).astype(BF)

    def outputs():
        yc[...] = xy_arrive(1)

    choose(0)
    gather_run(x_copies, [functools.partial(choose, s) for s in range(1, layers)] + [outputs])
    for copy in enc_loads:
        copy.wait()

    def x_copy(n, s):
        return pltpu.make_async_remote_copy(
            xs.at[n, s], xr.at[n, s], x_out.at[n, s], x_arr.at[n, s], device_id=beside
        )

    def pack(dense, n, s):
        both = dot(sel[s], dense)
        low, high = both[0:SLOTS, 0:BLOCK], both[SLOTS : 2 * SLOTS, BLOCK : 2 * BLOCK]
        keep[n, s] = jnp.where(x_lo == 0, low, high)
        xs[n, s] = jnp.where(x_lo == 0, high, low).astype(BF)
        x_copy(n, s).start()

    def z_copy(n, g, d):
        peer = lax.rem(z + d, nz)
        return pltpu.make_async_remote_copy(
            zs.at[n, g, peer], zr.at[n, g, z], z_out.at[n, g], z_arr.at[n, g], device_id=along(d)
        )

    def c_copy(n, g, d):
        where = cz.at[n, g, x_lo, z]
        return pltpu.make_async_remote_copy(where, where, c_out.at[n, g], c_arr.at[n, g], device_id=along(d))

    def cx_copy(n, g, half_of):
        where = cz.at[n, g, half_of]
        return pltpu.make_async_remote_copy(where, where, cx_out.at[n, g], cx_arr.at[n, g], device_id=beside)

    def all_along(copy, n, g):
        def one(d, carry):
            copy(n, g, d).start()
            return carry

        lax.fori_loop(1, nz, one, 0)

    def wait_along(sem, n, g):
        where = zr.at[n, g, pl.ds(0, nz - 1)]
        pltpu.make_async_copy(where, where, sem.at[n, g]).wait()

    def z_send(n, g, members):
        for i, s in enumerate(members):
            x_copy(n, s).wait_recv()
            total = keep[n, s] + xr[n, s].astype(F32)
            zs[n, g, :, i] = total.astype(BF).reshape(nz, shard, BLOCK)
        all_along(z_copy, n, g)
        zr[n, g, z] = zs[n, g, z]

    def z_total(n, g):
        wait_along(z_arr, n, g)
        return jnp.sum(zr[n, g].astype(F32), axis=0)

    def c_pass(n, g):
        wait_along(c_arr, n, g)
        cx_copy(n, g, x_lo).start()

    def blocks(n, g, i):
        return [cz[n, g, b, :, i].reshape(SLOTS, BLOCK) for b in range(2)]

    def unpack(two, dst, s):
        zero = jnp.zeros((SLOTS, BLOCK), BF)
        wide = jnp.concatenate(
            [jnp.concatenate([two[0], zero], axis=1), jnp.concatenate([zero, two[1]], axis=1)], axis=0
        )
        dst[:, s * lats : (s + 1) * lats] = dot(selt[s], wide).astype(BF)

    up = [(0, 1), (2, 3)]
    down = [(3, 2), (1, 0)]

    for s in range(layers):
        dense = dot(xg[:, first(s) : first(s) + span], encp[s]).astype(BF)
        pack(dense, 0, s)
    for g, members in enumerate(up):
        z_send(0, g, members)
    for g, members in enumerate(up):
        total = z_total(0, g)
        for i, s in enumerate(members):
            bias = jnp.where(x_lo == 0, bias_in[s : s + 1, 0:BLOCK], bias_in[s : s + 1, BLOCK : 2 * BLOCK])
            pre = total[i] + bias
            small = jnp.exp(-jnp.abs(pre))
            cz[0, g, x_lo, z, i] = (jnp.maximum(pre, 0.0) + jnp.log1p(small)).astype(BF)
            slope[s] = jnp.where(pre >= 0, 1.0, small) / (1.0 + small)
        all_along(c_copy, 0, g)
    for g in range(2):
        c_pass(0, g)
    for copy in dec_loads:
        copy.wait()

    def codes(g):
        cx_copy(0, g, 1 - x_lo).wait_recv()
        for i, s in enumerate(up[g]):
            unpack(blocks(0, g, i), cd, s)

    tiles = [min(layers, ((n + 1) * LANE - 1) // dl + 1) for n in range(width // LANE)]
    groups = []
    for n, count in enumerate(tiles):
        if groups and groups[-1][2] == count:
            groups[-1][1] = n + 1
        else:
            groups.append([n, n + 1, count])

    def decode(hh, out, c):
        base = pl.ds(pl.multiple_of(hh * half, 16), half)
        for lo, hi, count in groups:
            if cuts[c][0] <= lo * LANE < cuts[c][1]:
                lanes = slice(lo * LANE, hi * LANE)
                part = dot(cd[base, 0 : count * lats], dcat[lanes, 0 : count * lats], ((1,), (1,)))
                out[:, lanes] = part.astype(out.dtype)

    def lanes_of(c):
        return pl.ds(cuts[c][0], cuts[c][1] - cuts[c][0])

    hm_copies = [
        pltpu.make_async_remote_copy(
            hm_s.at[:, lanes_of(c)], hm_r.at[:, lanes_of(c)], hm_sem.at[0, c], hm_sem.at[1, c], device_id=mate
        )
        for c in range(nc)
    ]

    def mine(offset, c):
        return ho[local(offset), lanes_of(c)] + hm_r[local(offset), lanes_of(c)].astype(F32)

    def sums(to, count, buf_s, buf_r, send, recv):
        return [
            [
                pltpu.make_async_remote_copy(
                    buf_s.at[i, :, lanes_of(c)], buf_r.at[i, :, lanes_of(c)], send.at[i, c], recv.at[i, c], device_id=to
                )
                for c in range(nc)
            ]
            for i in range(count)
        ]

    a_copies = sums(to_a, na, ra_s, ra_r, rs_as, rs_ar)
    b_copies = sums(to_b, nb, rb_s, rb_r, rs_bs, rs_br)

    def forward(copies, buf_s, buf_r, i, offset, c):
        part = mine(offset, c)
        if i:
            copies[i - 1][c].wait_recv()
            part = part + buf_r[i - 1, :, lanes_of(c)].astype(F32)
        buf_s[i, :, lanes_of(c)] = part.astype(BF)
        copies[i][c].start()

    early = [c for c in range(nc) if max(n for lo, _, n in groups if lo * LANE < cuts[c][1]) <= len(up[0])]
    codes(0)
    for c in early:
        decode(1 - core, hm_s, c)
        hm_copies[c].start()
        decode(core, ho, c)
    codes(1)
    for i in range(na):
        if i == 0:
            for c in range(nc):
                if c not in early:
                    decode(1 - core, hm_s, c)
                    hm_copies[c].start()
        for c in range(nc):
            if i == 0:
                if c not in early:
                    decode(core, ho, c)
                hm_copies[c].wait_recv()
            forward(a_copies, ra_s, ra_r, i, na - i, c)
            if i < nb:
                forward(b_copies, rb_s, rb_r, i, i - nb, c)
    fx_copies = []
    for c in range(nc):
        total = mine(0, c)
        a_copies[na - 1][c].wait_recv()
        total = total + ra_r[na - 1, :, lanes_of(c)].astype(F32)
        if nb:
            b_copies[nb - 1][c].wait_recv()
            total = total + rb_r[nb - 1, :, lanes_of(c)].astype(F32)
        fx_s[:, lanes_of(c)] = total.astype(BF)
        fx_copies.append(
            pltpu.make_async_remote_copy(
                fx_s.at[:, lanes_of(c)], fx_r.at[:, lanes_of(c)], fx_sem.at[0, c], fx_sem.at[1, c], device_id=partner
            )
        )
        fx_copies[c].start()

    e_copies = gather_copies(eg, 1)
    for c in range(nc):
        fx_copies[c].wait_recv()
        lanes = lanes_of(c)
        whole = fx_s[:, lanes].astype(F32) + fx_r[:, lanes].astype(F32)
        eg[own, lanes] = (whole - yc[:, lanes].astype(F32)).astype(BF)
        gather_start(e_copies, c)

        @pl.when(owner)
        def _():
            recb[:, lanes] = whole.astype(BF)

    rec_copy = pltpu.make_async_remote_copy(recb, recb, rec_sem.at[0], rec_sem.at[1], device_id=mate)

    @pl.when(owner)
    def _():
        rec_copy.start()

    def turn(buf, out, n):
        out[n * LANE : (n + 1) * LANE, :] = buf[:, n * LANE : (n + 1) * LANE].T

    def turn_inputs(i):
        for n in range(width // LANE):
            if n % na == i:
                turn(xg, xt, n)

    gather_run(e_copies, [functools.partial(turn_inputs, i) for i in range(na)])

    for group in down:
        for s in group:
            low = dl * s // LANE * LANE
            dense = dot(eg[:, low:width], dcat[low:width, s * lats : (s + 1) * lats]).astype(BF)
            pack(dense, 1, s)

    def decoder_grad(t):
        out = dot(et[t * dl : (t + 1) * dl, :], cd[:, 0 : (t + 1) * lats])
        for s in range(t + 1):
            dg_ref[t * (t + 1) // 2 + s] = out[:, s * lats : (s + 1) * lats].astype(BF)

    for g, members in enumerate(down):
        z_send(1, g, members)
    for n in range(width // LANE):
        turn(eg, et, n)
    decoder_grad(0)
    for g, members in enumerate(down):
        total = z_total(1, g)
        for i, s in enumerate(members):
            cz[1, g, x_lo, z, i] = (total[i] * slope[s]).astype(BF)
        all_along(c_copy, 1, g)
    decoder_grad(1)
    decoder_grad(2)
    for g in range(2):
        c_pass(1, g)
    decoder_grad(3)

    for g, members in enumerate(down):
        cx_copy(1, g, 1 - x_lo).wait_recv()
        for i, s in enumerate(members):
            two = blocks(1, g, i)
            unpack(two, pgd, s)
            for b in range(2):
                bg_ref[s : s + 1, b * BLOCK : (b + 1) * BLOCK] = jnp.sum(two[b].astype(F32), axis=0, keepdims=True)
            eg_ref[s] = dot(xt[s * dl : (s + 1) * dl, :], pgd[:, s * lats : (s + 1) * lats]).astype(BF)

    @pl.when(owner)
    def _():
        rec_copy.wait_send()

    @pl.when(jnp.logical_not(owner))
    def _():
        rec_copy.wait_recv()

    take = jnp.where(iota((rows, chunk), 1) == iota((rows, chunk), 0) + rows * core, 1.0, 0.0).astype(BF)
    rec_ref[...] = dot(take, recb[...]).astype(BF)

    for n in range(2):
        xy_copy(n, mate, core).wait_send()

        @pl.when(jnp.logical_not(owner))
        def _():
            xy_copy(n, mate, 1 - core).wait_send()

    for copy in hm_copies + fx_copies:
        copy.wait_send()
    for group in a_copies + b_copies:
        for copy in group:
            copy.wait_send()
    gather_end(x_copies)
    gather_end(e_copies)
    for n in range(2):
        for s in range(layers):
            x_copy(n, s).wait_send()
        for g in range(2):
            wait_along(z_out, n, g)
            wait_along(c_out, n, g)
            cx_copy(n, g, x_lo).wait_send()


def step(sizes, layer_inputs, layer_outputs, encoder, encoder_bias, decoder, active_blocks):
    layers, dl, lats, rows, ny, nl, chunk = sizes
    width = layers * dl
    places = 2 * ny * chunk
    na, nb = ny // 2, max(1, ny // 2 - 1)
    nz = nl // 2
    shard = SLOTS // nz
    pairs = decoder.shape[0]
    vmem, dma = pltpu.VMEM, pltpu.SemaphoreType.DMA
    ring = (chunk, width)
    scratch = [
        vmem((places, width), BF),
        vmem((places, width), BF),
        vmem((width, places), BF),
        vmem((width, places), BF),
        vmem((places, layers * lats), BF),
        vmem((places, layers * lats), BF),
        vmem((layers, 3 * LANE, lats), BF),
        vmem((width, layers * lats), BF),
        vmem((layers, 2 * SLOTS, places), BF),
        vmem((layers, places, 2 * SLOTS), BF),
        vmem((2, 32, width), BF),
        vmem((2, 2, 32, width), BF),
        vmem((2, layers, SLOTS, BLOCK), BF),
        vmem((2, layers, SLOTS, BLOCK), BF),
        vmem((2, layers, SLOTS, BLOCK), F32),
        vmem((2, 2, nz, layers // 2, shard, BLOCK), BF),
        vmem((2, 2, nz, layers // 2, shard, BLOCK), BF),
        vmem((2, 2, 2, nz, layers // 2, shard, BLOCK), BF),
        vmem((layers, shard, BLOCK), F32),
        vmem((places // 2, width), BF),
        vmem((places // 2, width), BF),
        vmem((places // 2, width), F32),
        vmem((na,) + ring, BF),
        vmem((na,) + ring, BF),
        vmem((nb,) + ring, BF),
        vmem((nb,) + ring, BF),
        vmem(ring, BF),
        vmem(ring, BF),
        vmem(ring, BF),
        vmem(ring, BF),
        vmem((rows, layers, dl), BF),
        vmem((rows, layers, dl), BF),
        vmem((layers, active_blocks.shape[2], active_blocks.shape[1]), jnp.int32),
        vmem((layers, lats), F32),
        dma((4 + layers + pairs,)),
        dma((2, 2)),
        dma((2, 2)),
        dma((2, na, 3)),
        dma((2, na, 3)),
        dma((2, nb, 3)),
        dma((2, nb, 3)),
        dma((2, ny)),
        dma((2, ny)),
        dma((2, layers)),
        dma((2, layers)),
        dma((2, 2)),
        dma((2, 2)),
        dma((2, 2)),
        dma((2, 2)),
        dma((2, 2)),
        dma((2, 2)),
        dma((2, 3)),
        dma((na, 3)),
        dma((na, 3)),
        dma((nb, 3)),
        dma((nb, 3)),
        dma((2, 3)),
        dma((2,)),
    ]
    in_vmem = pl.BlockSpec(memory_space=pltpu.VMEM)
    rec, eg, bg, dg = pl.pallas_call(
        functools.partial(kernel, sizes),
        out_shape=(
            jax.ShapeDtypeStruct((rows, width), BF),
            jax.ShapeDtypeStruct((layers, dl, lats), BF),
            jax.ShapeDtypeStruct((layers, lats), F32),
            jax.ShapeDtypeStruct((pairs, dl, lats), BF),
        ),
        in_specs=[pl.BlockSpec(memory_space=pltpu.HBM)] * 6,
        out_specs=(in_vmem,) * 4,
        scratch_shapes=scratch,
        compiler_params=pltpu.CompilerParams(
            collective_id=0, has_side_effects=True, vmem_limit_bytes=56 * 1024 * 1024
        ),
    )(
        layer_inputs.transpose(2, 0, 1),
        layer_outputs,
        encoder,
        encoder_bias,
        decoder,
        active_blocks.transpose(0, 2, 1),
    )
    return rec.reshape(rows, layers, dl), eg, bg, dg


def solution(mesh):
    ny, nl = mesh.shape["layer"] // 4, mesh.shape["lat"]

    def local(layer_inputs, layer_outputs, encoder, encoder_bias, decoder, active_blocks):
        layers, dl, lats = encoder.shape
        rows = layer_outputs.shape[0]
        chunk = -(-2 * rows // 16) * 16
        sizes = (layers, dl, lats, rows, ny, nl, chunk)
        return step(sizes, layer_inputs, layer_outputs, encoder, encoder_bias, decoder, active_blocks)

    return jax.shard_map(
        local,
        mesh=mesh,
        in_specs=(
            P(None, "lat", "layer"),
            P("layer", None, "lat"),
            P(None, "lat", "layer"),
            P(None, "layer"),
            P(None, "lat", "layer"),
            P(),
        ),
        out_specs=(
            P("layer", None, "lat"),
            P(None, "lat", "layer"),
            P(None, "layer"),
            P(None, "lat", "layer"),
        ),
        check_vma=False,
    )
```

```python
import functools

import jax
import jax.numpy as jnp
from jax import lax
from jax.experimental import pallas as pl
from jax.experimental.pallas import tpu as pltpu
from jax.sharding import PartitionSpec as P

BLOCK = 128
ROWBLOCK = 32
MOST = 4
SLOTS = MOST * ROWBLOCK
TILE = 16
LANE = 128
BF, F32 = jnp.bfloat16, jnp.float32


def dot(a, b, dims=((1,), (0,))):
    return lax.dot_general(a, b, (dims, ((), ())), preferred_element_type=F32)


def iota(shape, dim):
    return lax.broadcasted_iota(jnp.int32, shape, dim)


def kernel(
    sizes,
    x_ref, y_ref, enc_ref, bias_ref, dec_ref, act_ref,
    rec_ref, eg_ref, bg_ref, dg_ref,
    xg, eg, xt, et, cd, pgd, encp, dcat, sel, selt,
    xy_s, xy_r, pk, rx, ck, pc, rc, pg, slope,
    hm_s, hm_r, ho, ra_s, ra_r, rb_s, rb_r, fx_s, fx_r, recb, yc, x_in, y_in, act_in, bias_in, bsum, egb, dgb,
    load_sem, xy_out, xy_sem, ag_out, ag_ar, ag_br, ag_mr,
    lat_s, lat_r, hm_sem, rs_out, rs_ar, rs_br, fx_out, fx_sem, rec_sem, out_sem,
):
    layers, dl, lats, rows, ny, nl, chunk = sizes
    width = layers * dl
    span = 3 * LANE
    half = ny * chunk
    places = 2 * half
    real = 2 * rows
    shard = 2 * SLOTS // nl
    na, nb = ny // 2, ny // 2 - 1

    me, q = lax.axis_index("layer"), lax.axis_index("lat")
    core = lax.rem(me, 2)
    y = lax.rem(me // 2, ny)
    h = me // (2 * ny)
    owner = core == h
    step = 1 - 2 * core

    def at(hh, yy, cc):
        return {"layer": (hh * ny + yy) * 2 + cc, "lat": q}

    mate, partner = at(h, y, 1 - core), at(1 - h, y, core)
    y_a, y_b = lax.rem(y + step + ny, ny), lax.rem(y - step + ny, ny)
    to_a, to_b = at(h, y_a, core), at(h, y_b, core)

    def place(hh, offset):
        slot = lax.rem(y + step * offset + 2 * ny, ny)
        return pl.ds(pl.multiple_of((hh * ny + slot) * chunk, 16), chunk)

    tiles = chunk // TILE

    def tile_of(hh, offset, c):
        slot = lax.rem(y + step * offset + 2 * ny, ny)
        return pl.ds(pl.multiple_of((hh * ny + slot) * chunk + c * TILE, TILE), TILE)

    def loop(count, body):
        def one(i, carry):
            body(i)
            return carry

        lax.fori_loop(0, count, one, 0)

    diagonal = at(1 - h, y, 1 - core)

    barrier = pltpu.get_barrier_semaphore()
    for peer in (mate, partner, diagonal, to_a, to_b):
        pl.semaphore_signal(barrier, inc=1, device_id=peer)

    def greet(d, carry):
        pl.semaphore_signal(barrier, inc=1, device_id={"layer": me, "lat": lax.rem(q + d, nl)})
        return carry

    lax.fori_loop(1, nl, greet, 0)

    loads = [
        pltpu.make_async_copy(x_ref, x_in, load_sem.at[0]),
        pltpu.make_async_copy(y_ref, y_in, load_sem.at[1]),
        pltpu.make_async_copy(act_ref, act_in, load_sem.at[2]),
        pltpu.make_async_copy(bias_ref, bias_in, load_sem.at[3]),
    ]
    for copy in loads:
        copy.start()
    encp[...] = jnp.zeros_like(encp)
    dcat[...] = jnp.zeros_like(dcat)

    def first(s):
        return min(dl * s // LANE * LANE, width - span)

    enc_loads, dec_loads = [], []
    for s in range(layers):
        where = encp.at[s, pl.ds(dl * s - first(s), dl)]
        enc_loads.append(pltpu.make_async_copy(enc_ref.at[s], where, load_sem.at[4 + s]))
    for t in range(layers):
        for s in range(t + 1):
            pair = t * (t + 1) // 2 + s
            where = dcat.at[pl.ds(dl * t, dl), pl.ds(lats * s, lats)]
            dec_loads.append(pltpu.make_async_copy(dec_ref.at[pair], where, load_sem.at[4 + layers + pair]))
    for copy in enc_loads + dec_loads:
        copy.start()

    def flat(ref):
        return jnp.concatenate([ref[:, s, :] for s in range(layers)], axis=1)

    pad = jnp.zeros((32 - rows, width), BF)
    loads[0].wait()
    xy_s[0] = jnp.concatenate([flat(x_in), pad], axis=0)
    loads[1].wait()
    xy_s[1] = jnp.concatenate([flat(y_in), pad], axis=0)

    pl.semaphore_wait(barrier, 5 + nl - 1)

    def xy_copy(n, to, w):
        return pltpu.make_async_remote_copy(
            xy_s.at[n], xy_r.at[n, w], xy_out.at[n, w], xy_sem.at[n, w], device_id=to
        )

    for n in range(2):
        @pl.when(owner)
        def _():
            xy_copy(n, partner, core).start()

        @pl.when(jnp.logical_not(owner))
        def _():
            xy_copy(n, mate, core).start()
            pltpu.make_async_remote_copy(
                xy_s.at[n], xy_r.at[n, core], xy_out.at[n, 1 - core], xy_sem.at[n, core], device_id=diagonal
            ).start()

    def merged(n):
        total = None
        for w in range(2):
            there, here = iota((chunk, 32), 0), iota((chunk, 32), 1)
            put = jnp.where((there == here + rows * w) & (here < rows), 1.0, 0.0).astype(BF)
            part = dot(put, xy_r[n, w])
            total = part if total is None else total + part
        return total.astype(BF)

    def xy_arrive(n):
        @pl.when(owner)
        def _():
            xy_r[n, core] = xy_s[n]
            xy_copy(n, mate, 1 - core).wait_recv()

        @pl.when(jnp.logical_not(owner))
        def _():
            for w in range(2):
                xy_copy(n, mate, w).wait_recv()

        return merged(n)

    def gather_copies(buf, n):
        def piece(to, offset, send, recv, c):
            where = buf.at[tile_of(core, offset, c)]
            return pltpu.make_async_remote_copy(where, where, send, recv, device_id=to)

        def a_out(i, c):
            return piece(to_a, -i, ag_out.at[n], ag_ar.at[n, i, c], c)

        def b_out(i, c):
            return piece(to_b, i, ag_out.at[n], ag_br.at[n, i, c], c)

        def a_in(i, c):
            return piece(to_a, -i - 1, ag_out.at[n], ag_ar.at[n, i, c], c)

        def b_in(i, c):
            return piece(to_b, i + 1, ag_out.at[n], ag_br.at[n, i, c], c)

        order = [0]
        for i in range(na):
            order.append(-i - 1)
            if i < nb:
                order.append(i + 1)

        def pass_on(j):
            where = buf.at[place(core, order[j])]
            return pltpu.make_async_remote_copy(where, where, ag_out.at[n], ag_mr.at[n, j], device_id=mate)

        def from_mate(j):
            where = buf.at[place(1 - core, -order[j])]
            return pltpu.make_async_remote_copy(where, where, ag_out.at[n], ag_mr.at[n, j], device_id=mate)

        return a_out, b_out, a_in, b_in, pass_on, from_mate

    def gather_start(copies, c):
        copies[0](0, c).start()
        if nb:
            copies[1](0, c).start()

    def gather_run(copies, extra):
        a_out, b_out, a_in, b_in, pass_on, from_mate = copies
        pass_on(0).start()
        j = 1
        for i in range(na):

            def advance(c):
                a_in(i, c).wait_recv()
                if i + 1 < na:
                    a_out(i + 1, c).start()
                if i < nb:
                    b_in(i, c).wait_recv()
                    if i + 1 < nb:
                        b_out(i + 1, c).start()

            loop(tiles, advance)
            for _ in range(2 if i < nb else 1):
                pass_on(j).start()
                j += 1
            if i < len(extra):
                extra[i]()
        for j in range(ny):
            from_mate(j).wait_recv()

    def sent(buf, rows_sent, sem):
        where = buf.at[pl.ds(0, rows_sent)]
        pltpu.make_async_copy(where, where, sem).wait()

    nr = act_in.shape[2]
    ii, jj = iota((nr, nr), 0), iota((nr, nr), 1)
    lane_place = iota((1, places), 1)
    lane_chip = jnp.zeros((1, places), jnp.int32)
    for c in range(1, 2 * ny):
        lane_chip = lane_chip + jnp.where(lane_place >= c * chunk, 1, 0)
    lane_in = lane_place - lane_chip * chunk
    lane_row = jnp.where(lane_in < real, lane_chip * real + lane_in, -2).astype(F32)
    m0, r1 = iota((SLOTS, nr), 0), iota((SLOTS, nr), 1)
    r0, m1 = iota((nr, SLOTS), 0), iota((nr, SLOTS), 1)
    col_rank = (m0 // ROWBLOCK).astype(F32)
    col_value = (ROWBLOCK * r1 + m0 % ROWBLOCK + 1).astype(F32)
    row_rank = (m1 // ROWBLOCK).astype(F32)
    row_value = (ROWBLOCK * r0 + m1 % ROWBLOCK + 1).astype(F32)
    chip_in = iota((chunk, SLOTS), 0)
    chip_row = jnp.where(chip_in < real, chip_in, -places).astype(F32)
    loads[2].wait()
    loads[3].wait()

    def choose(s):
        named = act_in[s]
        for b in range(2):
            hit_row = jnp.max(jnp.where(named == 2 * me + b, 1.0, 0.0), axis=0, keepdims=True)
            across = jnp.broadcast_to(hit_row, (nr, nr))
            hit = jnp.sum(jnp.where(ii == jj, across, 0.0), axis=1, keepdims=True)
            rank = jnp.sum(jnp.where(jj < ii, across, 0.0), axis=1, keepdims=True)
            rank_row = jnp.sum(jnp.where(ii < jj, jnp.broadcast_to(hit, (nr, nr)), 0.0), axis=0, keepdims=True)
            rank_row = jnp.where(hit_row > 0, rank_row, -1.0)
            rank = jnp.where(hit > 0, rank, -1.0)
            want = jnp.sum(jnp.where(rank_row == col_rank, col_value, 0.0), axis=1, keepdims=True) - 1.0
            want_row = jnp.sum(jnp.where(rank == row_rank, row_value, 0.0), axis=0, keepdims=True) - 1.0
            sel[s, b * SLOTS : (b + 1) * SLOTS, :] = jnp.where(want == lane_row, 1.0, 0.0).astype(BF)

            def chip(c):
                here = pl.ds(pl.multiple_of(c * chunk, TILE), chunk)
                selt[s, here, b * SLOTS : (b + 1) * SLOTS] = jnp.where(
                    chip_row == want_row - (c * real).astype(F32), 1.0, 0.0
                ).astype(BF)

            loop(2 * ny, chip)

    def outputs():
        yc[...] = xy_arrive(1)

    loop(layers, choose)

    own = place(core, 0)
    x_copies = gather_copies(xg, 0)
    xg[own, :] = xy_arrive(0)
    loop(tiles, functools.partial(gather_start, x_copies))

    gather_run(x_copies, [outputs])
    for copy in enc_loads:
        copy.wait()

    def lat_rows(j):
        return pl.ds(pl.multiple_of(j * shard, 16), shard)

    def scatter(src, dst, s, n):
        def one(d, carry):
            peer = lax.rem(q + d, nl)
            pltpu.make_async_remote_copy(
                src.at[s, lat_rows(peer)], dst.at[s, q], lat_s.at[n, s], lat_r.at[n, s],
                device_id={"layer": me, "lat": peer},
            ).start()
            return carry

        lax.fori_loop(1, nl, one, 0)
        dst[s, q] = src[s, lat_rows(q), :]

    def spread(buf, s, n):
        def one(d, carry):
            where = buf.at[s, lat_rows(q)]
            pltpu.make_async_remote_copy(
                where, where, lat_s.at[n, s], lat_r.at[n, s], device_id={"layer": me, "lat": lax.rem(q + d, nl)}
            ).start()
            return carry

        lax.fori_loop(1, nl, one, 0)

    def lat_wait(sem, s, n):
        where = ck.at[s, pl.ds(0, (nl - 1) * shard)]
        pltpu.make_async_copy(where, where, sem.at[n, s]).wait()

    def pack(dense, dst, s):
        both = dot(sel[s], dense)
        for b in range(2):
            part = slice(b * SLOTS, (b + 1) * SLOTS)
            dst[s, part, :] = both[part, b * BLOCK : (b + 1) * BLOCK].astype(BF)

    def lane_block(s):
        return pl.ds(pl.multiple_of(s * lats, LANE), lats)

    def encode(s):
        start = jnp.minimum(dl * s // LANE * LANE, width - span)
        dense = dot(xg[:, pl.ds(pl.multiple_of(start, LANE), span)], encp[s]).astype(BF)
        pack(dense, pk, s)
        scatter(pk, rx, s, 0)

    loop(layers, encode)

    def turn(src, out):
        def one(n):
            here = pl.ds(pl.multiple_of(n * LANE, LANE), LANE)
            out[here, :] = src[:, here].T

        loop(width // LANE, one)

    turn(xg, xt)

    b_of = q * shard // SLOTS
    def activate(s):
        lat_wait(lat_r, s, 0)
        total = jnp.sum(rx[s].astype(F32), axis=0)
        bias = bias_in[pl.ds(s, 1), :]
        pre = total + jnp.where(b_of == 0, bias[:, 0:BLOCK], bias[:, BLOCK : 2 * BLOCK])
        small = jnp.exp(-jnp.abs(pre))
        ck[s, lat_rows(q), :] = (jnp.maximum(pre, 0.0) + jnp.log1p(small)).astype(BF)
        slope[s] = jnp.where(pre >= 0, 1.0, small) / (1.0 + small)
        spread(ck, s, 1)

    loop(layers, activate)

    def unpack(src, dst, s):
        zero = jnp.zeros((SLOTS, BLOCK), BF)
        wide = jnp.concatenate(
            [
                jnp.concatenate([src[s, 0:SLOTS, :], zero], axis=1),
                jnp.concatenate([zero, src[s, SLOTS : 2 * SLOTS, :]], axis=1),
            ],
            axis=0,
        )
        dst[:, lane_block(s)] = dot(selt[s], wide).astype(BF)

    def codes(s):
        lat_wait(lat_r, s, 1)
        unpack(ck, cd, s)

    loop(layers, codes)

    for copy in dec_loads:
        copy.wait()

    groups = []
    for n in range(width // LANE):
        count = min(layers, ((n + 1) * LANE - 1) // dl + 1)
        if groups and groups[-1][2] == count:
            groups[-1][1] = n + 1
        else:
            groups.append([n, n + 1, count])

    hm_copy = pltpu.make_async_remote_copy(hm_s, hm_r, hm_sem.at[0], hm_sem.at[1], device_id=mate)

    def decode(j):
        hh = jnp.where(j == 0, 1 - core, core)
        base = pl.ds(pl.multiple_of(hh * half, TILE), half)
        for lo, hi, count in groups:
            lanes = slice(lo * LANE, hi * LANE)
            ho[:, lanes] = dot(cd[base, 0 : count * lats], dcat[lanes, 0 : count * lats], ((1,), (1,)))

        @pl.when(j == 0)
        def _():
            hm_s[...] = ho[...].astype(BF)
            hm_copy.start()

    loop(2, decode)
    hm_copy.wait_recv()

    def mine(offset, c):
        where = tile_of(0, offset, c)
        return ho[where, :] + hm_r[where, :].astype(F32)

    def small_tile(c):
        return pl.ds(pl.multiple_of(c * TILE, TILE), TILE)

    def a_copy(i, c):
        return pltpu.make_async_remote_copy(
            ra_s.at[i, small_tile(c)], ra_r.at[i, small_tile(c)], rs_out.at[0], rs_ar.at[i, c], device_id=to_a
        )

    def b_copy(i, c):
        return pltpu.make_async_remote_copy(
            rb_s.at[i, small_tile(c)], rb_r.at[i, small_tile(c)], rs_out.at[0], rs_br.at[i, c], device_id=to_b
        )

    def forward(copy, buf_s, buf_r, i, offset, c):
        part = mine(offset, c)
        if i:
            copy(i - 1, c).wait_recv()
            part = part + buf_r[i - 1, small_tile(c), :].astype(F32)
        buf_s[i, small_tile(c), :] = part.astype(BF)
        copy(i, c).start()

    for i in range(na):

        def both(c):
            forward(a_copy, ra_s, ra_r, i, na - i, c)
            if i < nb:
                forward(b_copy, rb_s, rb_r, i, i - nb, c)

        loop(tiles, both)

    def fx_copy(c):
        here = small_tile(c)
        return pltpu.make_async_remote_copy(
            fx_s.at[here], fx_r.at[here], fx_out.at[0], fx_sem.at[c], device_id=partner
        )

    def finish(c):
        here = small_tile(c)
        total = mine(0, c)
        a_copy(na - 1, c).wait_recv()
        total = total + ra_r[na - 1, here, :].astype(F32)
        if nb:
            b_copy(nb - 1, c).wait_recv()
            total = total + rb_r[nb - 1, here, :].astype(F32)
        fx_s[here, :] = total.astype(BF)
        fx_copy(c).start()

    loop(tiles, finish)

    e_copies = gather_copies(eg, 1)

    def differ(c):
        here = small_tile(c)
        fx_copy(c).wait_recv()
        whole = fx_s[here, :].astype(F32) + fx_r[here, :].astype(F32)
        eg[tile_of(core, 0, c), :] = (whole - yc[here, :].astype(F32)).astype(BF)
        gather_start(e_copies, c)
        ho[here, :] = whole

    loop(tiles, differ)

    @pl.when(owner)
    def _():
        recb[...] = ho[0:chunk, :].astype(BF)

    rec_copy = pltpu.make_async_remote_copy(recb, recb, rec_sem.at[0], rec_sem.at[1], device_id=mate)

    @pl.when(owner)
    def _():
        rec_copy.start()

    gather_run(e_copies, [])

    def out_copy(buf, ref, n, sem):
        return pltpu.make_async_copy(buf.at[n], ref.at[n], out_sem.at[sem])

    def back(s):
        dense = dot(eg[...], dcat[:, lane_block(s)]).astype(BF)
        pack(dense, pc, s)
        scatter(pc, rc, s, 2)

    loop(layers, back)
    turn(eg, et)

    def decoder_grad(pair):
        t = jnp.int32(0)
        for n in range(1, layers):
            t = t + jnp.where(pair >= n * (n + 1) // 2, 1, 0)
        s = pair - t * (t + 1) // 2
        out = dot(et[pl.ds(pl.multiple_of(t * dl, TILE), dl), :], cd[:, lane_block(s)])
        dgb[pair] = out.astype(BF)
        out_copy(dgb, dg_ref, pair, layers + pair).start()

    pairs = dg_ref.shape[0]
    loop(pairs // 3, decoder_grad)

    def settle(s):
        lat_wait(lat_r, s, 2)
        total = jnp.sum(rc[s].astype(F32), axis=0)
        pg[s, lat_rows(q), :] = (total * slope[s]).astype(BF)
        spread(pg, s, 3)

    loop(layers, settle)
    loop(pairs - pairs // 3, lambda n: decoder_grad(n + pairs // 3))

    def encoder_grad(s):
        lat_wait(lat_r, s, 3)
        unpack(pg, pgd, s)
        for b in range(2):
            bsum[s, :, b * BLOCK : (b + 1) * BLOCK] = jnp.sum(
                pg[s, b * SLOTS : (b + 1) * SLOTS, :].astype(F32), axis=0, keepdims=True
            )
        egb[s] = dot(xt[pl.ds(pl.multiple_of(s * dl, TILE), dl), :], pgd[:, lane_block(s)]).astype(BF)
        out_copy(egb, eg_ref, s, s).start()

    loop(layers, encoder_grad)
    for s in range(layers):
        bg_ref[s : s + 1, :] = bsum[s]

    @pl.when(owner)
    def _():
        rec_copy.wait_send()

    @pl.when(jnp.logical_not(owner))
    def _():
        rec_copy.wait_recv()

    take = jnp.where(iota((rows, chunk), 1) == iota((rows, chunk), 0) + rows * core, 1.0, 0.0).astype(BF)
    out = dot(take, recb[...]).astype(BF)
    for t in range(layers):
        rec_ref[:, t, :] = out[:, t * dl : (t + 1) * dl]

    for n in range(2):
        xy_copy(n, mate, core).wait_send()

        @pl.when(jnp.logical_not(owner))
        def _():
            xy_copy(n, mate, 1 - core).wait_send()

    loop(layers, lambda s: out_copy(egb, eg_ref, s, s).wait())
    loop(pairs, lambda n: out_copy(dgb, dg_ref, n, layers + n).wait())
    hm_copy.wait_send()
    sent(xg, chunk, fx_out.at[0])
    sent(xg, (na + nb) * chunk, rs_out.at[0])
    for n in range(2):
        sent(xg, (na + nb + ny) * chunk, ag_out.at[n])
    for n in range(4):
        for s in range(layers):
            lat_wait(lat_s, s, n)


def hand_over(*refs):
    count = (len(refs) - 1) // 2
    sem = refs[-1]
    copies = []
    for n in range(count):
        src, dst = refs[n], refs[count + n]
        parts = src.shape[0] if n in (1, 3) else 1
        for p in range(parts):
            pair = (src.at[p], dst.at[p]) if parts > 1 else (src, dst)
            copies.append(pltpu.make_async_copy(*pair, sem.at[len(copies)]))
    for copy in copies:
        copy.start()
    for copy in copies:
        copy.wait()


def step(sizes, layer_inputs, layer_outputs, encoder, encoder_bias, decoder, active_blocks):
    layers, dl, lats, rows, ny, nl, chunk = sizes
    width = layers * dl
    places = 2 * ny * chunk
    na, nb = ny // 2, max(1, ny // 2 - 1)
    shard = 2 * SLOTS // nl
    pairs = decoder.shape[0]
    vmem, dma = pltpu.VMEM, pltpu.SemaphoreType.DMA
    ring, tiles = (chunk, width), chunk // TILE
    scratch = [
        vmem((places, width), BF),
        vmem((places, width), BF),
        vmem((width, places), BF),
        vmem((width, places), BF),
        vmem((places, layers * lats), BF),
        vmem((places, layers * lats), BF),
        vmem((layers, 3 * LANE, lats), BF),
        vmem((width, layers * lats), BF),
        vmem((layers, 2 * SLOTS, places), BF),
        vmem((layers, places, 2 * SLOTS), BF),
        vmem((2, 32, width), BF),
        vmem((2, 2, 32, width), BF),
        vmem((layers, 2 * SLOTS, BLOCK), BF),
        vmem((layers, nl, shard, BLOCK), BF),
        vmem((layers, 2 * SLOTS, BLOCK), BF),
        vmem((layers, 2 * SLOTS, BLOCK), BF),
        vmem((layers, nl, shard, BLOCK), BF),
        vmem((layers, 2 * SLOTS, BLOCK), BF),
        vmem((layers, shard, BLOCK), F32),
        vmem((places // 2, width), BF),
        vmem((places // 2, width), BF),
        vmem((places // 2, width), F32),
        vmem((na,) + ring, BF),
        vmem((na,) + ring, BF),
        vmem((nb,) + ring, BF),
        vmem((nb,) + ring, BF),
        vmem(ring, BF),
        vmem(ring, BF),
        vmem(ring, BF),
        vmem(ring, BF),
        vmem((rows, layers, dl), BF),
        vmem((rows, layers, dl), BF),
        vmem((layers, active_blocks.shape[2], active_blocks.shape[1]), jnp.int32),
        vmem((layers, lats), F32),
        vmem((layers, 1, lats), F32),
        vmem((layers, dl, lats), BF),
        vmem((pairs, dl, lats), BF),
        dma((4 + layers + pairs,)),
        dma((2, 2)),
        dma((2, 2)),
        dma((2,)),
        dma((2, na, tiles)),
        dma((2, nb, tiles)),
        dma((2, ny)),
        dma((4, layers)),
        dma((4, layers)),
        dma((2,)),
        dma((1,)),
        dma((na, tiles)),
        dma((nb, tiles)),
        dma((1,)),
        dma((tiles,)),
        dma((2,)),
        dma((layers + pairs,)),
    ]
    in_vmem = pl.BlockSpec(memory_space=pltpu.VMEM)
    hbm = pl.BlockSpec(memory_space=pltpu.HBM)
    made = pl.pallas_call(
        functools.partial(kernel, sizes),
        out_shape=(
            jax.ShapeDtypeStruct((rows, layers, dl), BF),
            jax.ShapeDtypeStruct((layers, dl, lats), BF),
            jax.ShapeDtypeStruct((layers, lats), F32),
            jax.ShapeDtypeStruct((pairs, dl, lats), BF),
        ),
        in_specs=[hbm] * 6,
        out_specs=(in_vmem, hbm, in_vmem, hbm),
        scratch_shapes=scratch,
        compiler_params=pltpu.CompilerParams(
            collective_id=0, has_side_effects=True, vmem_limit_bytes=56 * 1024 * 1024
        ),
    )(
        layer_inputs.transpose(2, 0, 1),
        layer_outputs,
        encoder,
        encoder_bias,
        decoder,
        active_blocks.transpose(0, 2, 1),
    )
    return pl.pallas_call(
        hand_over,
        out_shape=tuple(jax.ShapeDtypeStruct(v.shape, v.dtype) for v in made),
        in_specs=[hbm] * 4,
        out_specs=(hbm,) * 4,
        scratch_shapes=[dma((layers + pairs + 2,))],
        compiler_params=pltpu.CompilerParams(vmem_limit_bytes=56 * 1024 * 1024),
    )(*made)


def solution(mesh):
    ny, nl = mesh.shape["layer"] // 4, mesh.shape["lat"]

    def local(layer_inputs, layer_outputs, encoder, encoder_bias, decoder, active_blocks):
        layers, dl, lats = encoder.shape
        rows = layer_outputs.shape[0]
        chunk = -(-2 * rows // 16) * 16
        sizes = (layers, dl, lats, rows, ny, nl, chunk)
        return step(sizes, layer_inputs, layer_outputs, encoder, encoder_bias, decoder, active_blocks)

    return jax.shard_map(
        local,
        mesh=mesh,
        in_specs=(
            P(None, "lat", "layer"),
            P("layer", None, "lat"),
            P(None, "lat", "layer"),
            P(None, "layer"),
            P(None, "lat", "layer"),
            P(),
        ),
        out_specs=(
            P("layer", None, "lat"),
            P(None, "lat", "layer"),
            P(None, "layer"),
            P(None, "lat", "layer"),
        ),
        check_vma=False,
    )
```

```python
import functools

import jax
import jax.numpy as jnp
from jax import lax
from jax.experimental import pallas as pl
from jax.experimental.pallas import tpu as pltpu
from jax.sharding import PartitionSpec as P

BLOCK = 128
ROWBLOCK = 32
MOST = 4
SLOTS = MOST * ROWBLOCK
TILE = 16
LANE = 128
BF, F32 = jnp.bfloat16, jnp.float32


def dot(a, b, dims=((1,), (0,))):
    return lax.dot_general(a, b, (dims, ((), ())), preferred_element_type=F32)


def iota(shape, dim):
    return lax.broadcasted_iota(jnp.int32, shape, dim)


def kernel(
    sizes,
    x_ref, y_ref, enc_ref, bias_ref, dec_ref, act_ref,
    rec_ref, eg_ref, bg_ref, dg_ref,
    xg, eg, xt, et, cd, pgd, encp, dcat, dturn, sel, selt,
    xy_s, xy_r, pk, rx, ck, pc, rc, pg, slope,
    hm_s, hm_r, ho, ra_s, ra_r, rb_s, rb_r, fx_s, fx_r, recb, yc, x_in, y_in, act_in, bias_in, bsum, egb, dgb,
    load_sem, xy_out, xy_sem, ag_out, ag_ar, ag_br, ag_mr,
    lat_s, lat_r, hm_sem, rs_out, rs_ar, rs_br, fx_out, fx_sem, rec_sem, out_sem,
):
    layers, dl, lats, rows, ny, nl, chunk = sizes
    width = layers * dl
    span = 3 * LANE
    half = ny * chunk
    places = 2 * half
    real = 2 * rows
    shard = 2 * SLOTS // nl
    na, nb = ny // 2, ny // 2 - 1

    me, q = lax.axis_index("layer"), lax.axis_index("lat")
    core = lax.rem(me, 2)
    y = lax.rem(me // 2, ny)
    h = me // (2 * ny)
    owner = core == h
    step = 1 - 2 * core

    def at(hh, yy, cc):
        return {"layer": (hh * ny + yy) * 2 + cc, "lat": q}

    mate, partner = at(h, y, 1 - core), at(1 - h, y, core)
    y_a, y_b = lax.rem(y + step + ny, ny), lax.rem(y - step + ny, ny)
    to_a, to_b = at(h, y_a, core), at(h, y_b, core)

    def place(hh, offset):
        slot = lax.rem(y + step * offset + 2 * ny, ny)
        return pl.ds(pl.multiple_of((hh * ny + slot) * chunk, 16), chunk)

    tiles = chunk // TILE

    def tile_of(hh, offset, c):
        slot = lax.rem(y + step * offset + 2 * ny, ny)
        return pl.ds(pl.multiple_of((hh * ny + slot) * chunk + c * TILE, TILE), TILE)

    def loop(count, body):
        def one(i, carry):
            body(i)
            return carry

        lax.fori_loop(0, count, one, 0)

    diagonal = at(1 - h, y, 1 - core)

    barrier = pltpu.get_barrier_semaphore()
    for peer in (mate, partner, diagonal, to_a, to_b):
        pl.semaphore_signal(barrier, inc=1, device_id=peer)

    def greet(d, carry):
        pl.semaphore_signal(barrier, inc=1, device_id={"layer": me, "lat": lax.rem(q + d, nl)})
        return carry

    lax.fori_loop(1, nl, greet, 0)

    loads = [
        pltpu.make_async_copy(x_ref, x_in, load_sem.at[0]),
        pltpu.make_async_copy(y_ref, y_in, load_sem.at[1]),
        pltpu.make_async_copy(act_ref, act_in, load_sem.at[2]),
        pltpu.make_async_copy(bias_ref, bias_in, load_sem.at[3]),
    ]
    for copy in loads:
        copy.start()
    encp[...] = jnp.zeros_like(encp)
    dcat[...] = jnp.zeros_like(dcat)

    def first(s):
        return min(dl * s // LANE * LANE, width - span)

    enc_loads, dec_loads = [], []
    for s in range(layers):
        where = encp.at[s, pl.ds(dl * s - first(s), dl)]
        enc_loads.append(pltpu.make_async_copy(enc_ref.at[s], where, load_sem.at[4 + s]))
    for t in range(layers):
        for s in range(t + 1):
            pair = t * (t + 1) // 2 + s
            where = dcat.at[pl.ds(dl * t, dl), pl.ds(lats * s, lats)]
            dec_loads.append(pltpu.make_async_copy(dec_ref.at[pair], where, load_sem.at[4 + layers + pair]))
    for copy in enc_loads + dec_loads:
        copy.start()

    def flat(ref):
        return jnp.concatenate([ref[:, s, :] for s in range(layers)], axis=1)

    pad = jnp.zeros((32 - rows, width), BF)
    loads[0].wait()
    xy_s[0] = jnp.concatenate([flat(x_in), pad], axis=0)
    pl.semaphore_wait(barrier, 5 + nl - 1)

    def xy_copy(n, to, w):
        return pltpu.make_async_remote_copy(
            xy_s.at[n], xy_r.at[n, w], xy_out.at[n, w], xy_sem.at[n, w], device_id=to
        )

    for n in range(2):
        if n:
            loads[1].wait()
            xy_s[1] = jnp.concatenate([flat(y_in), pad], axis=0)

        @pl.when(owner)
        def _():
            xy_copy(n, partner, core).start()

        @pl.when(jnp.logical_not(owner))
        def _():
            xy_copy(n, mate, core).start()
            pltpu.make_async_remote_copy(
                xy_s.at[n], xy_r.at[n, core], xy_out.at[n, 1 - core], xy_sem.at[n, core], device_id=diagonal
            ).start()

    def merged(n):
        total = None
        for w in range(2):
            there, here = iota((chunk, 32), 0), iota((chunk, 32), 1)
            put = jnp.where((there == here + rows * w) & (here < rows), 1.0, 0.0).astype(BF)
            part = dot(put, xy_r[n, w])
            total = part if total is None else total + part
        return total.astype(BF)

    def xy_arrive(n):
        @pl.when(owner)
        def _():
            xy_r[n, core] = xy_s[n]
            xy_copy(n, mate, 1 - core).wait_recv()

        @pl.when(jnp.logical_not(owner))
        def _():
            for w in range(2):
                xy_copy(n, mate, w).wait_recv()

        return merged(n)

    def gather_copies(buf, n):
        def piece(to, offset, send, recv, c):
            where = buf.at[tile_of(core, offset, c)]
            return pltpu.make_async_remote_copy(where, where, send, recv, device_id=to)

        def a_out(i, c):
            return piece(to_a, -i, ag_out.at[n], ag_ar.at[n, i, c], c)

        def b_out(i, c):
            return piece(to_b, i, ag_out.at[n], ag_br.at[n, i, c], c)

        def a_in(i, c):
            return piece(to_a, -i - 1, ag_out.at[n], ag_ar.at[n, i, c], c)

        def b_in(i, c):
            return piece(to_b, i + 1, ag_out.at[n], ag_br.at[n, i, c], c)

        order = [0]
        for i in range(na):
            order.append(-i - 1)
            if i < nb:
                order.append(i + 1)

        def pass_on(j):
            where = buf.at[place(core, order[j])]
            return pltpu.make_async_remote_copy(where, where, ag_out.at[n], ag_mr.at[n, j], device_id=mate)

        def from_mate(j):
            where = buf.at[place(1 - core, -order[j])]
            return pltpu.make_async_remote_copy(where, where, ag_out.at[n], ag_mr.at[n, j], device_id=mate)

        return a_out, b_out, a_in, b_in, pass_on, from_mate

    def gather_start(copies, c):
        copies[0](0, c).start()
        if nb:
            copies[1](0, c).start()

    def gather_run(copies, extra):
        a_out, b_out, a_in, b_in, pass_on, from_mate = copies
        pass_on(0).start()
        j = 1
        for i in range(na):

            def advance(c):
                a_in(i, c).wait_recv()
                if i + 1 < na:
                    a_out(i + 1, c).start()
                if i < nb:
                    b_in(i, c).wait_recv()
                    if i + 1 < nb:
                        b_out(i + 1, c).start()

            loop(tiles, advance)
            for _ in range(2 if i < nb else 1):
                pass_on(j).start()
                j += 1
            if i < len(extra):
                extra[i]()
        for j in range(ny):
            from_mate(j).wait_recv()

    def sent(buf, rows_sent, sem):
        where = buf.at[pl.ds(0, rows_sent)]
        pltpu.make_async_copy(where, where, sem).wait()

    nr = act_in.shape[2]
    ii, jj = iota((nr, nr), 0), iota((nr, nr), 1)
    lane_place = iota((1, places), 1)
    lane_chip = jnp.zeros((1, places), jnp.int32)
    for c in range(1, 2 * ny):
        lane_chip = lane_chip + jnp.where(lane_place >= c * chunk, 1, 0)
    lane_in = lane_place - lane_chip * chunk
    lane_row = jnp.where(lane_in < real, lane_chip * real + lane_in, -2).astype(F32)
    m0, r1 = iota((SLOTS, nr), 0), iota((SLOTS, nr), 1)
    r0, m1 = iota((nr, SLOTS), 0), iota((nr, SLOTS), 1)
    col_rank = (m0 // ROWBLOCK).astype(F32)
    col_value = (ROWBLOCK * r1 + m0 % ROWBLOCK + 1).astype(F32)
    row_rank = (m1 // ROWBLOCK).astype(F32)
    row_value = (ROWBLOCK * r0 + m1 % ROWBLOCK + 1).astype(F32)
    chip_in = iota((chunk, SLOTS), 0)
    chip_row = jnp.where(chip_in < real, chip_in, -places).astype(F32)
    loads[2].wait()
    loads[3].wait()

    def choose(s):
        named = act_in[s]
        for b in range(2):
            hit_row = jnp.max(jnp.where(named == 2 * me + b, 1.0, 0.0), axis=0, keepdims=True)
            across = jnp.broadcast_to(hit_row, (nr, nr))
            hit = jnp.sum(jnp.where(ii == jj, across, 0.0), axis=1, keepdims=True)
            rank = jnp.sum(jnp.where(jj < ii, across, 0.0), axis=1, keepdims=True)
            rank_row = jnp.sum(jnp.where(ii < jj, jnp.broadcast_to(hit, (nr, nr)), 0.0), axis=0, keepdims=True)
            rank_row = jnp.where(hit_row > 0, rank_row, -1.0)
            rank = jnp.where(hit > 0, rank, -1.0)
            want = jnp.sum(jnp.where(rank_row == col_rank, col_value, 0.0), axis=1, keepdims=True) - 1.0
            want_row = jnp.sum(jnp.where(rank == row_rank, row_value, 0.0), axis=0, keepdims=True) - 1.0
            sel[s, b * SLOTS : (b + 1) * SLOTS, :] = jnp.where(want == lane_row, 1.0, 0.0).astype(BF)

            def chip(c):
                here = pl.ds(pl.multiple_of(c * chunk, TILE), chunk)
                selt[s, here, b * SLOTS : (b + 1) * SLOTS] = jnp.where(
                    chip_row == want_row - (c * real).astype(F32), 1.0, 0.0
                ).astype(BF)

            loop(2 * ny, chip)

    def outputs():
        yc[...] = xy_arrive(1)

    loop(layers, choose)

    own = place(core, 0)
    x_copies = gather_copies(xg, 0)
    xg[own, :] = xy_arrive(0)
    loop(tiles, functools.partial(gather_start, x_copies))

    def turn(src, out, lo, hi):
        def one(n):
            here = pl.ds(pl.multiple_of((n + lo) * LANE, LANE), LANE)
            out[here, :] = src[:, here].T

        loop(hi - lo, one)

    def turn_part(src, out, i):
        count = src.shape[1] // LANE
        turn(src, out, count * i // na, count * (i + 1) // na)

    for copy in dec_loads:
        copy.wait()
    gather_run(x_copies, [functools.partial(turn_part, dcat, dturn, i) for i in range(na)])
    outputs()
    for copy in enc_loads:
        copy.wait()

    def lat_rows(j):
        return pl.ds(pl.multiple_of(j * shard, 16), shard)

    nz = nl // 2

    def peer_of(d):
        j = (d - 1) // 2
        away = nz // 2 + (j + 1) // 2 * (1 - 2 * lax.rem(j, 2))
        there = lax.rem(q // nz + d, 2)
        return there * nz + lax.rem(lax.rem(q, nz) + away, nz)

    def scatter(src, dst, s, n):
        def one(d, carry):
            peer = peer_of(d)
            pltpu.make_async_remote_copy(
                src.at[s, lat_rows(peer)], dst.at[s, q], lat_s.at[n, s], lat_r.at[n, s],
                device_id={"layer": me, "lat": peer},
            ).start()
            return carry

        lax.fori_loop(1, nl, one, 0)
        dst[s, q] = src[s, lat_rows(q), :]

    def spread(buf, s, n):
        def one(d, carry):
            where = buf.at[s, lat_rows(q)]
            pltpu.make_async_remote_copy(
                where, where, lat_s.at[n, s], lat_r.at[n, s], device_id={"layer": me, "lat": peer_of(d)}
            ).start()
            return carry

        lax.fori_loop(1, nl, one, 0)

    def lat_wait(sem, s, n):
        where = ck.at[s, pl.ds(0, (nl - 1) * shard)]
        pltpu.make_async_copy(where, where, sem.at[n, s]).wait()

    def pack(dense, dst, s):
        both = dot(sel[s], dense)
        for b in range(2):
            part = slice(b * SLOTS, (b + 1) * SLOTS)
            dst[s, part, :] = both[part, b * BLOCK : (b + 1) * BLOCK].astype(BF)

    def lane_block(s):
        return pl.ds(pl.multiple_of(s * lats, LANE), lats)

    def encode(s):
        start = jnp.minimum(dl * s // LANE * LANE, width - span)
        dense = dot(xg[:, pl.ds(pl.multiple_of(start, LANE), span)], encp[s]).astype(BF)
        pack(dense, pk, s)
        scatter(pk, rx, s, 0)

    loop(layers, encode)

    b_of = q * shard // SLOTS
    def activate(s):
        lat_wait(lat_r, s, 0)
        total = jnp.sum(rx[s].astype(F32), axis=0)
        bias = bias_in[pl.ds(s, 1), :]
        pre = total + jnp.where(b_of == 0, bias[:, 0:BLOCK], bias[:, BLOCK : 2 * BLOCK])
        small = jnp.exp(-jnp.abs(pre))
        ck[s, lat_rows(q), :] = (jnp.maximum(pre, 0.0) + jnp.log1p(small)).astype(BF)
        slope[s] = jnp.where(pre >= 0, 1.0, small) / (1.0 + small)
        spread(ck, s, 1)

    loop(layers, activate)

    def unpack(src, dst, s):
        zero = jnp.zeros((SLOTS, BLOCK), BF)
        wide = jnp.concatenate(
            [
                jnp.concatenate([src[s, 0:SLOTS, :], zero], axis=1),
                jnp.concatenate([zero, src[s, SLOTS : 2 * SLOTS, :]], axis=1),
            ],
            axis=0,
        )
        dst[:, lane_block(s)] = dot(selt[s], wide).astype(BF)

    def codes(s):
        lat_wait(lat_r, s, 1)
        unpack(ck, cd, s)

    loop(layers, codes)

    groups = []
    for n in range(width // LANE):
        count = min(layers, ((n + 1) * LANE - 1) // dl + 1)
        if groups and groups[-1][2] == count:
            groups[-1][1] = n + 1
        else:
            groups.append([n, n + 1, count])

    hm_copy = pltpu.make_async_remote_copy(hm_s, hm_r, hm_sem.at[0], hm_sem.at[1], device_id=mate)

    def decode(j):
        hh = jnp.where(j == 0, 1 - core, core)
        base = pl.ds(pl.multiple_of(hh * half, TILE), half)
        for lo, hi, count in groups:
            lanes = slice(lo * LANE, hi * LANE)
            ho[:, lanes] = dot(cd[base, 0 : count * lats], dturn[0 : count * lats, lanes])

        @pl.when(j == 0)
        def _():
            hm_s[...] = ho[...].astype(BF)
            hm_copy.start()

    loop(2, decode)
    hm_copy.wait_recv()

    def mine(offset, c):
        where = tile_of(0, offset, c)
        return ho[where, :] + hm_r[where, :].astype(F32)

    def small_tile(c):
        return pl.ds(pl.multiple_of(c * TILE, TILE), TILE)

    def a_copy(i, c):
        return pltpu.make_async_remote_copy(
            ra_s.at[i, small_tile(c)], ra_r.at[i, small_tile(c)], rs_out.at[0], rs_ar.at[i, c], device_id=to_a
        )

    def b_copy(i, c):
        return pltpu.make_async_remote_copy(
            rb_s.at[i, small_tile(c)], rb_r.at[i, small_tile(c)], rs_out.at[0], rs_br.at[i, c], device_id=to_b
        )

    def forward(copy, buf_s, buf_r, i, offset, c):
        part = mine(offset, c)
        if i:
            copy(i - 1, c).wait_recv()
            part = part + buf_r[i - 1, small_tile(c), :].astype(F32)
        buf_s[i, small_tile(c), :] = part.astype(BF)
        copy(i, c).start()

    for i in range(na):

        def both(c):
            forward(a_copy, ra_s, ra_r, i, na - i, c)
            if i < nb:
                forward(b_copy, rb_s, rb_r, i, i - nb, c)

        loop(tiles, both)
        turn_part(xg, xt, i)

    def fx_copy(c):
        here = small_tile(c)
        return pltpu.make_async_remote_copy(
            fx_s.at[here], fx_r.at[here], fx_out.at[0], fx_sem.at[c], device_id=partner
        )

    def finish(c):
        here = small_tile(c)
        total = mine(0, c)
        a_copy(na - 1, c).wait_recv()
        total = total + ra_r[na - 1, here, :].astype(F32)
        if nb:
            b_copy(nb - 1, c).wait_recv()
            total = total + rb_r[nb - 1, here, :].astype(F32)
        fx_s[here, :] = total.astype(BF)
        fx_copy(c).start()

    loop(tiles, finish)

    e_copies = gather_copies(eg, 1)

    def differ(c):
        here = small_tile(c)
        fx_copy(c).wait_recv()
        whole = fx_s[here, :].astype(F32) + fx_r[here, :].astype(F32)
        eg[tile_of(core, 0, c), :] = (whole - yc[here, :].astype(F32)).astype(BF)
        gather_start(e_copies, c)
        ho[here, :] = whole

    loop(tiles, differ)

    @pl.when(owner)
    def _():
        recb[...] = ho[0:chunk, :].astype(BF)

    rec_copy = pltpu.make_async_remote_copy(recb, recb, rec_sem.at[0], rec_sem.at[1], device_id=mate)

    @pl.when(owner)
    def _():
        rec_copy.start()

    gather_run(e_copies, [])

    def out_copy(buf, ref, n, sem):
        return pltpu.make_async_copy(buf.at[n], ref.at[n], out_sem.at[sem])

    def back(s):
        dense = dot(eg[...], dcat[:, lane_block(s)]).astype(BF)
        pack(dense, pc, s)
        scatter(pc, rc, s, 2)

    loop(layers, back)
    turn(eg, et, 0, width // LANE)

    def decoder_grad(pair):
        t = jnp.int32(0)
        for n in range(1, layers):
            t = t + jnp.where(pair >= n * (n + 1) // 2, 1, 0)
        s = pair - t * (t + 1) // 2
        out = dot(et[pl.ds(pl.multiple_of(t * dl, TILE), dl), :], cd[:, lane_block(s)])
        dgb[pair] = out.astype(BF)
        out_copy(dgb, dg_ref, pair, layers + pair).start()

    pairs = dg_ref.shape[0]

    def settle(s):
        lat_wait(lat_r, s, 2)
        total = jnp.sum(rc[s].astype(F32), axis=0)
        pg[s, lat_rows(q), :] = (total * slope[s]).astype(BF)
        spread(pg, s, 3)

    loop(layers, settle)
    loop(pairs, decoder_grad)

    @pl.when(owner)
    def _():
        rec_copy.wait_send()

    @pl.when(jnp.logical_not(owner))
    def _():
        rec_copy.wait_recv()

    take = jnp.where(iota((rows, chunk), 1) == iota((rows, chunk), 0) + rows * core, 1.0, 0.0).astype(BF)
    out = dot(take, recb[...]).astype(BF)
    for t in range(layers):
        rec_ref[:, t, :] = out[:, t * dl : (t + 1) * dl]


    def encoder_grad(s):
        lat_wait(lat_r, s, 3)
        unpack(pg, pgd, s)
        for b in range(2):
            bsum[s, :, b * BLOCK : (b + 1) * BLOCK] = jnp.sum(
                pg[s, b * SLOTS : (b + 1) * SLOTS, :].astype(F32), axis=0, keepdims=True
            )
        egb[s] = dot(xt[pl.ds(pl.multiple_of(s * dl, TILE), dl), :], pgd[:, lane_block(s)]).astype(BF)
        out_copy(egb, eg_ref, s, s).start()

    loop(layers, encoder_grad)
    for s in range(layers):
        bg_ref[s : s + 1, :] = bsum[s]

    for n in range(2):
        xy_copy(n, mate, core).wait_send()

        @pl.when(jnp.logical_not(owner))
        def _():
            xy_copy(n, mate, 1 - core).wait_send()

    loop(layers, lambda s: out_copy(egb, eg_ref, s, s).wait())
    loop(pairs, lambda n: out_copy(dgb, dg_ref, n, layers + n).wait())
    hm_copy.wait_send()
    sent(xg, chunk, fx_out.at[0])
    sent(xg, (na + nb) * chunk, rs_out.at[0])
    for n in range(2):
        sent(xg, (na + nb + ny) * chunk, ag_out.at[n])
    for n in range(4):
        for s in range(layers):
            lat_wait(lat_s, s, n)


def hand_over(*refs):
    count = (len(refs) - 2) // 3
    come, go = refs[-2:]
    copies = []
    for n in range(count):
        src, dst, mid = refs[n], refs[count + n], refs[2 * count + n]
        parts = src.shape[0] if n in (1, 3) else 1
        for p in range(parts):
            a, b, c = (src.at[p], mid.at[p], dst.at[p]) if parts > 1 else (src, mid, dst)
            k = len(copies)
            copies.append((pltpu.make_async_copy(a, b, come.at[k]), pltpu.make_async_copy(b, c, go.at[k])))
    for first, _ in copies:
        first.start()
    for first, second in copies:
        first.wait()
        second.start()
    for _, second in copies:
        second.wait()


def step(sizes, layer_inputs, layer_outputs, encoder, encoder_bias, decoder, active_blocks):
    layers, dl, lats, rows, ny, nl, chunk = sizes
    width = layers * dl
    places = 2 * ny * chunk
    na, nb = ny // 2, max(1, ny // 2 - 1)
    shard = 2 * SLOTS // nl
    pairs = decoder.shape[0]
    vmem, dma = pltpu.VMEM, pltpu.SemaphoreType.DMA
    ring, tiles = (chunk, width), chunk // TILE
    scratch = [
        vmem((places, width), BF),
        vmem((places, width), BF),
        vmem((width, places), BF),
        vmem((width, places), BF),
        vmem((places, layers * lats), BF),
        vmem((places, layers * lats), BF),
        vmem((layers, 3 * LANE, lats), BF),
        vmem((width, layers * lats), BF),
        vmem((layers * lats, width), BF),
        vmem((layers, 2 * SLOTS, places), BF),
        vmem((layers, places, 2 * SLOTS), BF),
        vmem((2, 32, width), BF),
        vmem((2, 2, 32, width), BF),
        vmem((layers, 2 * SLOTS, BLOCK), BF),
        vmem((layers, nl, shard, BLOCK), BF),
        vmem((layers, 2 * SLOTS, BLOCK), BF),
        vmem((layers, 2 * SLOTS, BLOCK), BF),
        vmem((layers, nl, shard, BLOCK), BF),
        vmem((layers, 2 * SLOTS, BLOCK), BF),
        vmem((layers, shard, BLOCK), F32),
        vmem((places // 2, width), BF),
        vmem((places // 2, width), BF),
        vmem((places // 2, width), F32),
        vmem((na,) + ring, BF),
        vmem((na,) + ring, BF),
        vmem((nb,) + ring, BF),
        vmem((nb,) + ring, BF),
        vmem(ring, BF),
        vmem(ring, BF),
        vmem(ring, BF),
        vmem(ring, BF),
        vmem((rows, layers, dl), BF),
        vmem((rows, layers, dl), BF),
        vmem((layers, active_blocks.shape[2], active_blocks.shape[1]), jnp.int32),
        vmem((layers, lats), F32),
        vmem((layers, 1, lats), F32),
        vmem((layers, dl, lats), BF),
        vmem((pairs, dl, lats), BF),
        dma((4 + layers + pairs,)),
        dma((2, 2)),
        dma((2, 2)),
        dma((2,)),
        dma((2, na, tiles)),
        dma((2, nb, tiles)),
        dma((2, ny)),
        dma((4, layers)),
        dma((4, layers)),
        dma((2,)),
        dma((1,)),
        dma((na, tiles)),
        dma((nb, tiles)),
        dma((1,)),
        dma((tiles,)),
        dma((2,)),
        dma((layers + pairs,)),
    ]
    in_vmem = pl.BlockSpec(memory_space=pltpu.VMEM)
    hbm = pl.BlockSpec(memory_space=pltpu.HBM)
    made = pl.pallas_call(
        functools.partial(kernel, sizes),
        out_shape=(
            jax.ShapeDtypeStruct((rows, layers, dl), BF),
            jax.ShapeDtypeStruct((layers, dl, lats), BF),
            jax.ShapeDtypeStruct((layers, lats), F32),
            jax.ShapeDtypeStruct((pairs, dl, lats), BF),
        ),
        in_specs=[hbm] * 6,
        out_specs=(in_vmem, hbm, in_vmem, hbm),
        scratch_shapes=scratch,
        compiler_params=pltpu.CompilerParams(
            collective_id=0, has_side_effects=True, vmem_limit_bytes=56 * 1024 * 1024
        ),
    )(
        layer_inputs.transpose(2, 0, 1),
        layer_outputs,
        encoder,
        encoder_bias,
        decoder,
        active_blocks.transpose(0, 2, 1),
    )
    return pl.pallas_call(
        hand_over,
        out_shape=tuple(jax.ShapeDtypeStruct(v.shape, v.dtype) for v in made),
        in_specs=[hbm] * 4,
        out_specs=(hbm,) * 4,
        scratch_shapes=[vmem(v.shape, v.dtype) for v in made] + [dma((layers + pairs + 2,))] * 2,
        compiler_params=pltpu.CompilerParams(vmem_limit_bytes=56 * 1024 * 1024),
    )(*made)


def solution(mesh):
    ny, nl = mesh.shape["layer"] // 4, mesh.shape["lat"]

    def local(layer_inputs, layer_outputs, encoder, encoder_bias, decoder, active_blocks):
        layers, dl, lats = encoder.shape
        rows = layer_outputs.shape[0]
        chunk = -(-2 * rows // 16) * 16
        sizes = (layers, dl, lats, rows, ny, nl, chunk)
        return step(sizes, layer_inputs, layer_outputs, encoder, encoder_bias, decoder, active_blocks)

    return jax.shard_map(
        local,
        mesh=mesh,
        in_specs=(
            P(None, "lat", "layer"),
            P("layer", None, "lat"),
            P(None, "lat", "layer"),
            P(None, "layer"),
            P(None, "lat", "layer"),
            P(),
        ),
        out_specs=(
            P("layer", None, "lat"),
            P(None, "lat", "layer"),
            P(None, "layer"),
            P(None, "lat", "layer"),
        ),
        check_vma=False,
    )
```

```python
import functools

import jax
import jax.numpy as jnp
from jax import lax
from jax.experimental import pallas as pl
from jax.experimental.pallas import tpu as pltpu
from jax.sharding import PartitionSpec as P

BLOCK = 128
ROWBLOCK = 32
MOST = 4
SLOTS = MOST * ROWBLOCK
TILE = 16
LANE = 128
BF, F32 = jnp.bfloat16, jnp.float32


def dot(a, b, dims=((1,), (0,))):
    return lax.dot_general(a, b, (dims, ((), ())), preferred_element_type=F32)


def iota(shape, dim):
    return lax.broadcasted_iota(jnp.int32, shape, dim)


def kernel(
    sizes,
    x_ref, y_ref, enc_ref, bias_ref, dec_ref, act_ref,
    rec_ref, eg_ref, bg_ref, dg_ref,
    xg, eg, xt, et, cd, pgd, encp, dcat, dturn, sel, selt,
    xy_s, xy_r, pk, rx, ck, pc, rc, pg, slope,
    hm_s, hm_r, ho, ra_s, ra_r, rb_s, rb_r, fx_s, fx_r, recb, yc, x_in, y_in, act_in, bias_in, bsum, egb, dgb,
    load_sem, xy_out, xy_sem, ag_out, ag_ar, ag_br, ag_mr,
    lat_s, lat_r, hm_out, hm_sem, rs_out, rs_ar, rs_br, fx_out, fx_sem, rec_sem, out_sem,
):
    layers, dl, lats, rows, ny, nl, chunk = sizes
    width = layers * dl
    span = 3 * LANE
    half = ny * chunk
    places = 2 * half
    real = 2 * rows
    shard = 2 * SLOTS // nl
    na, nb = ny // 2, ny // 2 - 1

    me, q = lax.axis_index("layer"), lax.axis_index("lat")
    core = lax.rem(me, 2)
    y = lax.rem(me // 2, ny)
    h = me // (2 * ny)
    owner = core == h
    step = 1 - 2 * core

    def at(hh, yy, cc):
        return {"layer": (hh * ny + yy) * 2 + cc, "lat": q}

    mate, partner = at(h, y, 1 - core), at(1 - h, y, core)
    y_a, y_b = lax.rem(y + step + ny, ny), lax.rem(y - step + ny, ny)
    to_a, to_b = at(h, y_a, core), at(h, y_b, core)
    two_a = at(h, lax.rem(y + 2 * step + ny, ny), core)
    two_b = at(h, lax.rem(y - 2 * step + ny, ny), core)
    stages = na - 1

    def place(hh, offset):
        slot = lax.rem(y + step * offset + 2 * ny, ny)
        return pl.ds(pl.multiple_of((hh * ny + slot) * chunk, 16), chunk)

    tiles = chunk // TILE

    def tile_of(hh, offset, c):
        slot = lax.rem(y + step * offset + 2 * ny, ny)
        return pl.ds(pl.multiple_of((hh * ny + slot) * chunk + c * TILE, TILE), TILE)

    def loop(count, body):
        def one(i, carry):
            body(i)
            return carry

        lax.fori_loop(0, count, one, 0)

    diagonal = at(1 - h, y, 1 - core)

    barrier = pltpu.get_barrier_semaphore()
    for peer in (mate, partner, diagonal, to_a, to_b, two_a, two_b):
        pl.semaphore_signal(barrier, inc=1, device_id=peer)

    def greet(d, carry):
        pl.semaphore_signal(barrier, inc=1, device_id={"layer": me, "lat": lax.rem(q + d, nl)})
        return carry

    lax.fori_loop(1, nl, greet, 0)

    loads = [
        pltpu.make_async_copy(x_ref, x_in, load_sem.at[0]),
        pltpu.make_async_copy(y_ref, y_in, load_sem.at[1]),
        pltpu.make_async_copy(act_ref, act_in, load_sem.at[2]),
        pltpu.make_async_copy(bias_ref, bias_in, load_sem.at[3]),
    ]
    for copy in loads:
        copy.start()
    encp[...] = jnp.zeros_like(encp)
    dcat[...] = jnp.zeros_like(dcat)

    def first(s):
        return min(dl * s // LANE * LANE, width - span)

    enc_loads, dec_loads = [], []
    for s in range(layers):
        where = encp.at[s, pl.ds(dl * s - first(s), dl)]
        enc_loads.append(pltpu.make_async_copy(enc_ref.at[s], where, load_sem.at[4 + s]))
    for t in range(layers):
        for s in range(t + 1):
            pair = t * (t + 1) // 2 + s
            where = dcat.at[pl.ds(dl * t, dl), pl.ds(lats * s, lats)]
            dec_loads.append(pltpu.make_async_copy(dec_ref.at[pair], where, load_sem.at[4 + layers + pair]))
    for copy in enc_loads + dec_loads:
        copy.start()

    def flat(ref):
        return jnp.concatenate([ref[:, s, :] for s in range(layers)], axis=1)

    pad = jnp.zeros((32 - rows, width), BF)
    loads[0].wait()
    xy_s[0] = jnp.concatenate([flat(x_in), pad], axis=0)
    pl.semaphore_wait(barrier, 7 + nl - 1)

    def xy_copy(n, to, w):
        return pltpu.make_async_remote_copy(
            xy_s.at[n], xy_r.at[n, w], xy_out.at[n, w], xy_sem.at[n, w], device_id=to
        )

    for n in range(2):
        if n:
            loads[1].wait()
            xy_s[1] = jnp.concatenate([flat(y_in), pad], axis=0)

        @pl.when(owner)
        def _():
            xy_copy(n, partner, core).start()

        @pl.when(jnp.logical_not(owner))
        def _():
            xy_copy(n, mate, core).start()
            pltpu.make_async_remote_copy(
                xy_s.at[n], xy_r.at[n, core], xy_out.at[n, 1 - core], xy_sem.at[n, core], device_id=diagonal
            ).start()

    def merged(n):
        total = None
        for w in range(2):
            there, here = iota((chunk, 32), 0), iota((chunk, 32), 1)
            put = jnp.where((there == here + rows * w) & (here < rows), 1.0, 0.0).astype(BF)
            part = dot(put, xy_r[n, w])
            total = part if total is None else total + part
        return total.astype(BF)

    def xy_arrive(n):
        @pl.when(owner)
        def _():
            xy_r[n, core] = xy_s[n]
            xy_copy(n, mate, 1 - core).wait_recv()

        @pl.when(jnp.logical_not(owner))
        def _():
            for w in range(2):
                xy_copy(n, mate, w).wait_recv()

        return merged(n)

    def gather_copies(buf, n):
        def piece(to, offset, send, recv, c):
            where = buf.at[tile_of(core, offset, c)]
            return pltpu.make_async_remote_copy(where, where, send, recv, device_id=to)

        def a_out(i, c):
            if i == na - 1:
                return piece(two_a, 2 - na, ag_out.at[n], ag_ar.at[n, i, c], c)
            return piece(to_a, -i, ag_out.at[n], ag_ar.at[n, i, c], c)

        def b_out(i, c):
            return piece(to_b, i, ag_out.at[n], ag_br.at[n, i, c], c)

        def a_in(i, c):
            return piece(to_a, -i - 1, ag_out.at[n], ag_ar.at[n, i, c], c)

        def b_in(i, c):
            return piece(to_b, i + 1, ag_out.at[n], ag_br.at[n, i, c], c)

        order = [0]
        for i in range(na):
            order.append(-i - 1)
            if i < nb:
                order.append(i + 1)

        def pass_on(j, c=None):
            where = buf.at[place(core, order[j]) if c is None else tile_of(core, order[j], c)]
            return pltpu.make_async_remote_copy(where, where, ag_out.at[n], ag_mr.at[n, j], device_id=mate)

        def from_mate(j):
            where = buf.at[place(1 - core, -order[j])]
            return pltpu.make_async_remote_copy(where, where, ag_out.at[n], ag_mr.at[n, j], device_id=mate)

        return a_out, b_out, a_in, b_in, pass_on, from_mate

    def start_a(copies, i, c):
        copies[0](i, c).start()
        if i == stages - 1:
            copies[0](na - 1, c).start()

    def gather_start(copies, c):
        start_a(copies, 0, c)
        copies[1](0, c).start()

    def gather_run(copies, extra):
        a_out, b_out, a_in, b_in, pass_on, from_mate = copies
        pass_on(0).start()
        for i in range(stages):
            last = i + 1 == stages

            def advance(c):
                a_in(i, c).wait_recv()
                if last:
                    pass_on(2 * i + 1, c).start()
                else:
                    start_a(copies, i + 1, c)
                b_in(i, c).wait_recv()
                if last:
                    pass_on(2 * i + 2, c).start()
                    a_in(na - 1, c).wait_recv()
                    pass_on(2 * i + 3, c).start()
                else:
                    b_out(i + 1, c).start()

            loop(tiles, advance)
            if not last:
                pass_on(2 * i + 1).start()
                pass_on(2 * i + 2).start()
            if i < len(extra):
                extra[i]()
        for j in range(ny):
            from_mate(j).wait_recv()

    def sent(buf, rows_sent, sem):
        where = buf.at[pl.ds(0, rows_sent)]
        pltpu.make_async_copy(where, where, sem).wait()

    nr = act_in.shape[2]
    ii, jj = iota((nr, nr), 0), iota((nr, nr), 1)
    lane_place = iota((1, places), 1)
    lane_chip = jnp.zeros((1, places), jnp.int32)
    for c in range(1, 2 * ny):
        lane_chip = lane_chip + jnp.where(lane_place >= c * chunk, 1, 0)
    lane_in = lane_place - lane_chip * chunk
    lane_row = jnp.where(lane_in < real, lane_chip * real + lane_in, -2).astype(F32)
    m0, r1 = iota((SLOTS, nr), 0), iota((SLOTS, nr), 1)
    r0, m1 = iota((nr, SLOTS), 0), iota((nr, SLOTS), 1)
    col_rank = (m0 // ROWBLOCK).astype(F32)
    col_value = (ROWBLOCK * r1 + m0 % ROWBLOCK + 1).astype(F32)
    row_rank = (m1 // ROWBLOCK).astype(F32)
    row_value = (ROWBLOCK * r0 + m1 % ROWBLOCK + 1).astype(F32)
    chip_in = iota((chunk, SLOTS), 0)
    chip_row = jnp.where(chip_in < real, chip_in, -places).astype(F32)
    loads[2].wait()
    loads[3].wait()

    def choose(s):
        named = act_in[s]
        for b in range(2):
            hit_row = jnp.max(jnp.where(named == 2 * me + b, 1.0, 0.0), axis=0, keepdims=True)
            across = jnp.broadcast_to(hit_row, (nr, nr))
            hit = jnp.sum(jnp.where(ii == jj, across, 0.0), axis=1, keepdims=True)
            rank = jnp.sum(jnp.where(jj < ii, across, 0.0), axis=1, keepdims=True)
            rank_row = jnp.sum(jnp.where(ii < jj, jnp.broadcast_to(hit, (nr, nr)), 0.0), axis=0, keepdims=True)
            rank_row = jnp.where(hit_row > 0, rank_row, -1.0)
            rank = jnp.where(hit > 0, rank, -1.0)
            want = jnp.sum(jnp.where(rank_row == col_rank, col_value, 0.0), axis=1, keepdims=True) - 1.0
            want_row = jnp.sum(jnp.where(rank == row_rank, row_value, 0.0), axis=0, keepdims=True) - 1.0
            sel[s, b * SLOTS : (b + 1) * SLOTS, :] = jnp.where(want == lane_row, 1.0, 0.0).astype(BF)

            def chip(c):
                here = pl.ds(pl.multiple_of(c * chunk, TILE), chunk)
                selt[s, here, b * SLOTS : (b + 1) * SLOTS] = jnp.where(
                    chip_row == want_row - (c * real).astype(F32), 1.0, 0.0
                ).astype(BF)

            loop(2 * ny, chip)

    def outputs():
        yc[...] = xy_arrive(1)

    loop(layers, choose)

    own = place(core, 0)
    x_copies = gather_copies(xg, 0)
    xg[own, :] = xy_arrive(0)
    loop(tiles, functools.partial(gather_start, x_copies))

    def turn(src, out, lo, hi):
        def one(n):
            here = pl.ds(pl.multiple_of((n + lo) * LANE, LANE), LANE)
            out[here, :] = src[:, here].T

        loop(hi - lo, one)

    def turn_part(src, out, i):
        count = src.shape[1] // LANE
        turn(src, out, count * i // stages, count * (i + 1) // stages)

    for copy in dec_loads:
        copy.wait()
    gather_run(x_copies, [functools.partial(turn_part, dcat, dturn, i) for i in range(stages)])
    outputs()
    for copy in enc_loads:
        copy.wait()

    def lat_rows(j):
        return pl.ds(pl.multiple_of(j * shard, 16), shard)

    nz = nl // 2

    def peer_of(d):
        j = (d - 1) // 2
        away = nz // 2 + (j + 1) // 2 * (1 - 2 * lax.rem(j, 2))
        there = lax.rem(q // nz + d, 2)
        return there * nz + lax.rem(lax.rem(q, nz) + away, nz)

    def scatter(src, dst, s, n):
        def one(d, carry):
            peer = peer_of(d)
            pltpu.make_async_remote_copy(
                src.at[s, lat_rows(peer)], dst.at[s, q], lat_s.at[n, s], lat_r.at[n, s],
                device_id={"layer": me, "lat": peer},
            ).start()
            return carry

        lax.fori_loop(1, nl, one, 0)
        dst[s, q] = src[s, lat_rows(q), :]

    def spread(buf, s, n):
        def one(d, carry):
            where = buf.at[s, lat_rows(q)]
            pltpu.make_async_remote_copy(
                where, where, lat_s.at[n, s], lat_r.at[n, s], device_id={"layer": me, "lat": peer_of(d)}
            ).start()
            return carry

        lax.fori_loop(1, nl, one, 0)

    def lat_wait(sem, s, n):
        where = ck.at[s, pl.ds(0, (nl - 1) * shard)]
        pltpu.make_async_copy(where, where, sem.at[n, s]).wait()

    def pack(dense, dst, s):
        both = dot(sel[s], dense)
        for b in range(2):
            part = slice(b * SLOTS, (b + 1) * SLOTS)
            dst[s, part, :] = both[part, b * BLOCK : (b + 1) * BLOCK].astype(BF)

    def lane_block(s):
        return pl.ds(pl.multiple_of(s * lats, LANE), lats)

    def encode(s):
        start = jnp.minimum(dl * s // LANE * LANE, width - span)
        dense = dot(xg[:, pl.ds(pl.multiple_of(start, LANE), span)], encp[s]).astype(BF)
        pack(dense, pk, s)
        scatter(pk, rx, s, 0)

    loop(layers, encode)

    b_of = q * shard // SLOTS
    def activate(s):
        lat_wait(lat_r, s, 0)
        total = jnp.sum(rx[s].astype(F32), axis=0)
        bias = bias_in[pl.ds(s, 1), :]
        pre = total + jnp.where(b_of == 0, bias[:, 0:BLOCK], bias[:, BLOCK : 2 * BLOCK])
        small = jnp.exp(-jnp.abs(pre))
        ck[s, lat_rows(q), :] = (jnp.maximum(pre, 0.0) + jnp.log1p(small)).astype(BF)
        slope[s] = jnp.where(pre >= 0, 1.0, small) / (1.0 + small)
        spread(ck, s, 1)

    loop(layers, activate)

    def unpack(src, dst, s):
        zero = jnp.zeros((SLOTS, BLOCK), BF)
        wide = jnp.concatenate(
            [
                jnp.concatenate([src[s, 0:SLOTS, :], zero], axis=1),
                jnp.concatenate([zero, src[s, SLOTS : 2 * SLOTS, :]], axis=1),
            ],
            axis=0,
        )
        dst[:, lane_block(s)] = dot(selt[s], wide).astype(BF)

    def codes(s):
        lat_wait(lat_r, s, 1)
        unpack(ck, cd, s)

    loop(layers, codes)

    groups = []
    for n in range(width // LANE):
        count = min(layers, ((n + 1) * LANE - 1) // dl + 1)
        if groups and groups[-1][2] == count:
            groups[-1][1] = n + 1
        else:
            groups.append([n, n + 1, count])

    uses = [na, na - 1, -nb]
    for i in range(1, nb):
        uses += [na - 1 - i, i - nb]
    uses.append(0)

    def hm_copy(offset, sign):
        where = place(0, sign * offset)
        return pltpu.make_async_remote_copy(
            hm_s.at[where], hm_r.at[where], hm_out.at[0], hm_sem.at[uses.index(offset)], device_id=mate
        )

    def decode(j):
        hh = jnp.where(j == 0, 1 - core, core)
        base = pl.ds(pl.multiple_of(hh * half, TILE), half)
        for lo, hi, count in groups:
            lanes = slice(lo * LANE, hi * LANE)
            ho[:, lanes] = dot(cd[base, 0 : count * lats], dturn[0 : count * lats, lanes])

        @pl.when(j == 0)
        def _():
            hm_s[...] = ho[...].astype(BF)
            for offset in uses:
                hm_copy(offset, -1).start()

    loop(2, decode)

    def mine(offset, c):
        where = tile_of(0, offset, c)
        return ho[where, :] + hm_r[where, :].astype(F32)

    def small_tile(c):
        return pl.ds(pl.multiple_of(c * TILE, TILE), TILE)

    def a_copy(i, c):
        return pltpu.make_async_remote_copy(
            ra_s.at[i, small_tile(c)],
            ra_r.at[i, small_tile(c)],
            rs_out.at[0],
            rs_ar.at[i, c],
            device_id=to_a if i else two_a,
        )

    def b_copy(i, c):
        return pltpu.make_async_remote_copy(
            rb_s.at[i, small_tile(c)], rb_r.at[i, small_tile(c)], rs_out.at[0], rs_br.at[i, c], device_id=to_b
        )

    def forward(copy, buf_s, buf_r, i, offset, earlier, c):
        part = mine(offset, c)
        for n in earlier:
            copy(n, c).wait_recv()
            part = part + buf_r[n, small_tile(c), :].astype(F32)
        buf_s[i, small_tile(c), :] = part.astype(BF)
        copy(i, c).start()

    def from_a(i):
        return [] if i < 2 else [0, 1] if i == 2 else [i - 1]

    for i in range(stages):
        now = [na, na - 1, -nb] if i == 0 else [na - 1 - i, i - nb]
        for offset in now:
            hm_copy(offset, 1).wait_recv()

        def both(c):
            if i == 0:
                forward(a_copy, ra_s, ra_r, 0, na, [], c)
            forward(a_copy, ra_s, ra_r, i + 1, na - 1 - i, from_a(i + 1), c)
            forward(b_copy, rb_s, rb_r, i, i - nb, [i - 1] if i else [], c)

        loop(tiles, both)
        turn_part(xg, xt, i)

    hm_copy(0, 1).wait_recv()

    def fx_copy(c):
        here = small_tile(c)
        return pltpu.make_async_remote_copy(
            fx_s.at[here], fx_r.at[here], fx_out.at[0], fx_sem.at[c], device_id=partner
        )

    def finish(c):
        here = small_tile(c)
        total = mine(0, c)
        for n in from_a(na):
            a_copy(n, c).wait_recv()
            total = total + ra_r[n, here, :].astype(F32)
        b_copy(nb - 1, c).wait_recv()
        total = total + rb_r[nb - 1, here, :].astype(F32)
        fx_s[here, :] = total.astype(BF)
        fx_copy(c).start()

    loop(tiles, finish)

    e_copies = gather_copies(eg, 1)

    def differ(c):
        here = small_tile(c)
        fx_copy(c).wait_recv()
        whole = fx_s[here, :].astype(F32) + fx_r[here, :].astype(F32)
        eg[tile_of(core, 0, c), :] = (whole - yc[here, :].astype(F32)).astype(BF)
        gather_start(e_copies, c)
        ho[here, :] = whole

    loop(tiles, differ)

    @pl.when(owner)
    def _():
        recb[...] = ho[0:chunk, :].astype(BF)

    rec_copy = pltpu.make_async_remote_copy(recb, recb, rec_sem.at[0], rec_sem.at[1], device_id=mate)

    @pl.when(owner)
    def _():
        rec_copy.start()

    gather_run(e_copies, [])

    def out_copy(buf, ref, n, sem):
        return pltpu.make_async_copy(buf.at[n], ref.at[n], out_sem.at[sem])

    def back(s):
        dense = dot(eg[...], dcat[:, lane_block(s)]).astype(BF)
        pack(dense, pc, s)
        scatter(pc, rc, s, 2)

    loop(layers, back)
    turn(eg, et, 0, width // LANE)

    def decoder_grad(pair):
        t = jnp.int32(0)
        for n in range(1, layers):
            t = t + jnp.where(pair >= n * (n + 1) // 2, 1, 0)
        s = pair - t * (t + 1) // 2
        out = dot(et[pl.ds(pl.multiple_of(t * dl, TILE), dl), :], cd[:, lane_block(s)])
        dgb[pair] = out.astype(BF)
        out_copy(dgb, dg_ref, pair, layers + pair).start()

    pairs = dg_ref.shape[0]

    def settle(s):
        lat_wait(lat_r, s, 2)
        total = jnp.sum(rc[s].astype(F32), axis=0)
        pg[s, lat_rows(q), :] = (total * slope[s]).astype(BF)
        spread(pg, s, 3)

    loop(layers, settle)
    loop(pairs, decoder_grad)

    @pl.when(owner)
    def _():
        rec_copy.wait_send()

    @pl.when(jnp.logical_not(owner))
    def _():
        rec_copy.wait_recv()

    take = jnp.where(iota((rows, chunk), 1) == iota((rows, chunk), 0) + rows * core, 1.0, 0.0).astype(BF)
    out = dot(take, recb[...]).astype(BF)
    for t in range(layers):
        rec_ref[:, t, :] = out[:, t * dl : (t + 1) * dl]


    def encoder_grad(s):
        lat_wait(lat_r, s, 3)
        unpack(pg, pgd, s)
        for b in range(2):
            bsum[s, :, b * BLOCK : (b + 1) * BLOCK] = jnp.sum(
                pg[s, b * SLOTS : (b + 1) * SLOTS, :].astype(F32), axis=0, keepdims=True
            )
        egb[s] = dot(xt[pl.ds(pl.multiple_of(s * dl, TILE), dl), :], pgd[:, lane_block(s)]).astype(BF)
        out_copy(egb, eg_ref, s, s).start()

    loop(layers, encoder_grad)
    for s in range(layers):
        bg_ref[s : s + 1, :] = bsum[s]

    for n in range(2):
        xy_copy(n, mate, core).wait_send()

        @pl.when(jnp.logical_not(owner))
        def _():
            xy_copy(n, mate, 1 - core).wait_send()

    loop(layers, lambda s: out_copy(egb, eg_ref, s, s).wait())
    loop(pairs, lambda n: out_copy(dgb, dg_ref, n, layers + n).wait())
    sent(hm_s, half, hm_out.at[0])
    sent(xg, chunk, fx_out.at[0])
    sent(xg, (na + nb) * chunk, rs_out.at[0])
    for n in range(2):
        sent(xg, (na + nb + ny) * chunk, ag_out.at[n])
    for n in range(4):
        for s in range(layers):
            lat_wait(lat_s, s, n)


def hand_over(*refs):
    count = (len(refs) - 2) // 3
    come, go = refs[-2:]
    copies = []
    for n in range(count):
        src, dst, mid = refs[n], refs[count + n], refs[2 * count + n]
        parts = src.shape[0] if n in (1, 3) else 1
        for p in range(parts):
            a, b, c = (src.at[p], mid.at[p], dst.at[p]) if parts > 1 else (src, mid, dst)
            k = len(copies)
            copies.append((pltpu.make_async_copy(a, b, come.at[k]), pltpu.make_async_copy(b, c, go.at[k])))
    for first, _ in copies:
        first.start()
    for first, second in copies:
        first.wait()
        second.start()
    for _, second in copies:
        second.wait()


def step(sizes, layer_inputs, layer_outputs, encoder, encoder_bias, decoder, active_blocks):
    layers, dl, lats, rows, ny, nl, chunk = sizes
    width = layers * dl
    places = 2 * ny * chunk
    na, nb = ny // 2, max(1, ny // 2 - 1)
    shard = 2 * SLOTS // nl
    pairs = decoder.shape[0]
    vmem, dma = pltpu.VMEM, pltpu.SemaphoreType.DMA
    ring, tiles = (chunk, width), chunk // TILE
    scratch = [
        vmem((places, width), BF),
        vmem((places, width), BF),
        vmem((width, places), BF),
        vmem((width, places), BF),
        vmem((places, layers * lats), BF),
        vmem((places, layers * lats), BF),
        vmem((layers, 3 * LANE, lats), BF),
        vmem((width, layers * lats), BF),
        vmem((layers * lats, width), BF),
        vmem((layers, 2 * SLOTS, places), BF),
        vmem((layers, places, 2 * SLOTS), BF),
        vmem((2, 32, width), BF),
        vmem((2, 2, 32, width), BF),
        vmem((layers, 2 * SLOTS, BLOCK), BF),
        vmem((layers, nl, shard, BLOCK), BF),
        vmem((layers, 2 * SLOTS, BLOCK), BF),
        vmem((layers, 2 * SLOTS, BLOCK), BF),
        vmem((layers, nl, shard, BLOCK), BF),
        vmem((layers, 2 * SLOTS, BLOCK), BF),
        vmem((layers, shard, BLOCK), F32),
        vmem((places // 2, width), BF),
        vmem((places // 2, width), BF),
        vmem((places // 2, width), F32),
        vmem((na,) + ring, BF),
        vmem((na,) + ring, BF),
        vmem((nb,) + ring, BF),
        vmem((nb,) + ring, BF),
        vmem(ring, BF),
        vmem(ring, BF),
        vmem(ring, BF),
        vmem(ring, BF),
        vmem((rows, layers, dl), BF),
        vmem((rows, layers, dl), BF),
        vmem((layers, active_blocks.shape[2], active_blocks.shape[1]), jnp.int32),
        vmem((layers, lats), F32),
        vmem((layers, 1, lats), F32),
        vmem((layers, dl, lats), BF),
        vmem((pairs, dl, lats), BF),
        dma((4 + layers + pairs,)),
        dma((2, 2)),
        dma((2, 2)),
        dma((2,)),
        dma((2, na, tiles)),
        dma((2, nb, tiles)),
        dma((2, ny)),
        dma((4, layers)),
        dma((4, layers)),
        dma((1,)),
        dma((ny,)),
        dma((1,)),
        dma((na, tiles)),
        dma((nb, tiles)),
        dma((1,)),
        dma((tiles,)),
        dma((2,)),
        dma((layers + pairs,)),
    ]
    in_vmem = pl.BlockSpec(memory_space=pltpu.VMEM)
    hbm = pl.BlockSpec(memory_space=pltpu.HBM)
    made = pl.pallas_call(
        functools.partial(kernel, sizes),
        out_shape=(
            jax.ShapeDtypeStruct((rows, layers, dl), BF),
            jax.ShapeDtypeStruct((layers, dl, lats), BF),
            jax.ShapeDtypeStruct((layers, lats), F32),
            jax.ShapeDtypeStruct((pairs, dl, lats), BF),
        ),
        in_specs=[hbm] * 6,
        out_specs=(in_vmem, hbm, in_vmem, hbm),
        scratch_shapes=scratch,
        compiler_params=pltpu.CompilerParams(
            collective_id=0, has_side_effects=True, vmem_limit_bytes=56 * 1024 * 1024
        ),
    )(
        layer_inputs.transpose(2, 0, 1),
        layer_outputs,
        encoder,
        encoder_bias,
        decoder,
        active_blocks.transpose(0, 2, 1),
    )
    return pl.pallas_call(
        hand_over,
        out_shape=tuple(jax.ShapeDtypeStruct(v.shape, v.dtype) for v in made),
        in_specs=[hbm] * 4,
        out_specs=(hbm,) * 4,
        scratch_shapes=[vmem(v.shape, v.dtype) for v in made] + [dma((layers + pairs + 2,))] * 2,
        compiler_params=pltpu.CompilerParams(vmem_limit_bytes=56 * 1024 * 1024),
    )(*made)


def solution(mesh):
    ny, nl = mesh.shape["layer"] // 4, mesh.shape["lat"]

    def local(layer_inputs, layer_outputs, encoder, encoder_bias, decoder, active_blocks):
        layers, dl, lats = encoder.shape
        rows = layer_outputs.shape[0]
        chunk = -(-2 * rows // 16) * 16
        sizes = (layers, dl, lats, rows, ny, nl, chunk)
        return step(sizes, layer_inputs, layer_outputs, encoder, encoder_bias, decoder, active_blocks)

    return jax.shard_map(
        local,
        mesh=mesh,
        in_specs=(
            P(None, "lat", "layer"),
            P("layer", None, "lat"),
            P(None, "lat", "layer"),
            P(None, "layer"),
            P(None, "lat", "layer"),
            P(),
        ),
        out_specs=(
            P("layer", None, "lat"),
            P(None, "lat", "layer"),
            P(None, "layer"),
            P(None, "lat", "layer"),
        ),
        check_vma=False,
    )
```

```python
import functools

import jax
import jax.numpy as jnp
from jax import lax
from jax.experimental import pallas as pl
from jax.experimental.pallas import tpu as pltpu
from jax.sharding import PartitionSpec as P

BLOCK = 128
ROWBLOCK = 32
MOST = 4
SLOTS = MOST * ROWBLOCK
TILE = 16
LANE = 128
BF, F32 = jnp.bfloat16, jnp.float32


def dot(a, b, dims=((1,), (0,))):
    return lax.dot_general(a, b, (dims, ((), ())), preferred_element_type=F32)


def iota(shape, dim):
    return lax.broadcasted_iota(jnp.int32, shape, dim)


def kernel(
    sizes,
    x_ref, y_ref, enc_ref, bias_ref, dec_ref, act_ref,
    rec_ref, eg_ref, bg_ref, dg_ref,
    xg, eg, xt, et, cd, pgd, encp, dcat, dturn, sel, selt,
    xy_s, xy_r, pk, rx, ck, pc, rc, pg, slope,
    hm_s, hm_r, ho, ra_s, ra_r, rb_s, rb_r, fx_s, fx_r, recb, yc, x_in, y_in, act_in, bias_in, bsum, egb, dgb,
    load_sem, xy_out, xy_sem, ag_out, ag_ar, ag_br, ag_mr,
    lat_s, lat_r, hm_out, hm_sem, rs_out, rs_ar, rs_br, fx_out, fx_sem, rec_sem, out_sem,
):
    layers, dl, lats, rows, ny, nl, chunk = sizes
    width = layers * dl
    span = 3 * LANE
    half = ny * chunk
    places = 2 * half
    real = 2 * rows
    shard = 2 * SLOTS // nl
    na, nb = ny // 2, ny // 2 - 1

    me, q = lax.axis_index("layer"), lax.axis_index("lat")
    core = lax.rem(me, 2)
    y = lax.rem(me // 2, ny)
    h = me // (2 * ny)
    owner = core == h
    step = 1 - 2 * core

    def at(hh, yy, cc):
        return {"layer": (hh * ny + yy) * 2 + cc, "lat": q}

    mate, partner = at(h, y, 1 - core), at(1 - h, y, core)
    y_a, y_b = lax.rem(y + step + ny, ny), lax.rem(y - step + ny, ny)
    to_a, to_b = at(h, y_a, core), at(h, y_b, core)
    two_a = at(h, lax.rem(y + 2 * step + ny, ny), core)
    two_b = at(h, lax.rem(y - 2 * step + ny, ny), core)
    stages = na - 1

    def place(hh, offset):
        slot = lax.rem(y + step * offset + 2 * ny, ny)
        return pl.ds(pl.multiple_of((hh * ny + slot) * chunk, 16), chunk)

    tiles = chunk // TILE

    def tile_of(hh, offset, c):
        slot = lax.rem(y + step * offset + 2 * ny, ny)
        return pl.ds(pl.multiple_of((hh * ny + slot) * chunk + c * TILE, TILE), TILE)

    def loop(count, body):
        def one(i, carry):
            body(i)
            return carry

        lax.fori_loop(0, count, one, 0)

    diagonal = at(1 - h, y, 1 - core)

    barrier = pltpu.get_barrier_semaphore()
    for peer in (mate, partner, diagonal, to_a, to_b, two_a, two_b):
        pl.semaphore_signal(barrier, inc=1, device_id=peer)

    def greet(d, carry):
        pl.semaphore_signal(barrier, inc=1, device_id={"layer": me, "lat": lax.rem(q + d, nl)})
        return carry

    lax.fori_loop(1, nl, greet, 0)

    loads = [
        pltpu.make_async_copy(x_ref, x_in, load_sem.at[0]),
        pltpu.make_async_copy(y_ref, y_in, load_sem.at[1]),
        pltpu.make_async_copy(act_ref, act_in, load_sem.at[2]),
        pltpu.make_async_copy(bias_ref, bias_in, load_sem.at[3]),
    ]
    for copy in loads:
        copy.start()
    encp[...] = jnp.zeros_like(encp)
    dcat[...] = jnp.zeros_like(dcat)

    def first(s):
        return min(dl * s // LANE * LANE, width - span)

    enc_loads, dec_loads = [], []
    for s in range(layers):
        where = encp.at[s, pl.ds(dl * s - first(s), dl)]
        enc_loads.append(pltpu.make_async_copy(enc_ref.at[s], where, load_sem.at[4 + s]))
    for t in range(layers):
        for s in range(t + 1):
            pair = t * (t + 1) // 2 + s
            where = dcat.at[pl.ds(dl * t, dl), pl.ds(lats * s, lats)]
            dec_loads.append(pltpu.make_async_copy(dec_ref.at[pair], where, load_sem.at[4 + layers + pair]))
    for copy in enc_loads + dec_loads:
        copy.start()

    def flat(ref):
        return jnp.concatenate([ref[:, s, :] for s in range(layers)], axis=1)

    pad = jnp.zeros((32 - rows, width), BF)
    loads[0].wait()
    xy_s[0] = jnp.concatenate([flat(x_in), pad], axis=0)
    pl.semaphore_wait(barrier, 7 + nl - 1)

    def xy_copy(n, to, w):
        return pltpu.make_async_remote_copy(
            xy_s.at[n], xy_r.at[n, w], xy_out.at[n, w], xy_sem.at[n, w], device_id=to
        )

    for n in range(2):
        if n:
            loads[1].wait()
            xy_s[1] = jnp.concatenate([flat(y_in), pad], axis=0)

        @pl.when(owner)
        def _():
            xy_copy(n, partner, core).start()

        @pl.when(jnp.logical_not(owner))
        def _():
            xy_copy(n, mate, core).start()
            pltpu.make_async_remote_copy(
                xy_s.at[n], xy_r.at[n, core], xy_out.at[n, 1 - core], xy_sem.at[n, core], device_id=diagonal
            ).start()

    def merged(n):
        total = None
        for w in range(2):
            there, here = iota((chunk, 32), 0), iota((chunk, 32), 1)
            put = jnp.where((there == here + rows * w) & (here < rows), 1.0, 0.0).astype(BF)
            part = dot(put, xy_r[n, w])
            total = part if total is None else total + part
        return total.astype(BF)

    def xy_arrive(n):
        @pl.when(owner)
        def _():
            xy_r[n, core] = xy_s[n]
            xy_copy(n, mate, 1 - core).wait_recv()

        @pl.when(jnp.logical_not(owner))
        def _():
            for w in range(2):
                xy_copy(n, mate, w).wait_recv()

        return merged(n)

    def gather_copies(buf, n):
        def piece(to, offset, send, recv, c):
            where = buf.at[tile_of(core, offset, c)]
            return pltpu.make_async_remote_copy(where, where, send, recv, device_id=to)

        def a_out(i, c):
            if i == na - 1:
                return piece(two_a, 2 - na, ag_out.at[n], ag_ar.at[n, i, c], c)
            return piece(to_a, -i, ag_out.at[n], ag_ar.at[n, i, c], c)

        def b_out(i, c):
            return piece(to_b, i, ag_out.at[n], ag_br.at[n, i, c], c)

        def a_in(i, c):
            return piece(to_a, -i - 1, ag_out.at[n], ag_ar.at[n, i, c], c)

        def b_in(i, c):
            return piece(to_b, i + 1, ag_out.at[n], ag_br.at[n, i, c], c)

        order = [0]
        for i in range(na):
            order.append(-i - 1)
            if i < nb:
                order.append(i + 1)

        def pass_on(j, c=None):
            where = buf.at[place(core, order[j]) if c is None else tile_of(core, order[j], c)]
            return pltpu.make_async_remote_copy(where, where, ag_out.at[n], ag_mr.at[n, j], device_id=mate)

        def from_mate(j):
            where = buf.at[place(1 - core, -order[j])]
            return pltpu.make_async_remote_copy(where, where, ag_out.at[n], ag_mr.at[n, j], device_id=mate)

        return a_out, b_out, a_in, b_in, pass_on, from_mate

    def start_a(copies, i, c):
        copies[0](i, c).start()
        if i == stages - 1:
            copies[0](na - 1, c).start()

    def gather_start(copies, c):
        start_a(copies, 0, c)
        copies[1](0, c).start()

    def gather_run(copies, extra):
        a_out, b_out, a_in, b_in, pass_on, from_mate = copies
        pass_on(0).start()
        for i in range(stages):
            last = i + 1 == stages

            def advance(c):
                a_in(i, c).wait_recv()
                if last:
                    pass_on(2 * i + 1, c).start()
                else:
                    start_a(copies, i + 1, c)
                b_in(i, c).wait_recv()
                if last:
                    pass_on(2 * i + 2, c).start()
                    a_in(na - 1, c).wait_recv()
                    pass_on(2 * i + 3, c).start()
                else:
                    b_out(i + 1, c).start()

            loop(tiles, advance)
            if not last:
                pass_on(2 * i + 1).start()
                pass_on(2 * i + 2).start()
            if i < len(extra):
                extra[i]()
        for j in range(ny):
            from_mate(j).wait_recv()

    def sent(buf, rows_sent, sem):
        where = buf.at[pl.ds(0, rows_sent)]
        pltpu.make_async_copy(where, where, sem).wait()

    nr = act_in.shape[2]
    ii, jj = iota((nr, nr), 0), iota((nr, nr), 1)
    lane_place = iota((1, places), 1)
    lane_chip = jnp.zeros((1, places), jnp.int32)
    for c in range(1, 2 * ny):
        lane_chip = lane_chip + jnp.where(lane_place >= c * chunk, 1, 0)
    lane_in = lane_place - lane_chip * chunk
    lane_row = jnp.where(lane_in < real, lane_chip * real + lane_in, -2).astype(F32)
    m0, r1 = iota((SLOTS, nr), 0), iota((SLOTS, nr), 1)
    r0, m1 = iota((nr, SLOTS), 0), iota((nr, SLOTS), 1)
    col_rank = (m0 // ROWBLOCK).astype(F32)
    col_value = (ROWBLOCK * r1 + m0 % ROWBLOCK + 1).astype(F32)
    row_rank = (m1 // ROWBLOCK).astype(F32)
    row_value = (ROWBLOCK * r0 + m1 % ROWBLOCK + 1).astype(F32)
    chip_in = iota((chunk, SLOTS), 0)
    chip_row = jnp.where(chip_in < real, chip_in, -places).astype(F32)
    loads[2].wait()
    loads[3].wait()

    def choose(s):
        named = act_in[s]
        for b in range(2):
            hit_row = jnp.max(jnp.where(named == 2 * me + b, 1.0, 0.0), axis=0, keepdims=True)
            across = jnp.broadcast_to(hit_row, (nr, nr))
            hit = jnp.sum(jnp.where(ii == jj, across, 0.0), axis=1, keepdims=True)
            rank = jnp.sum(jnp.where(jj < ii, across, 0.0), axis=1, keepdims=True)
            rank_row = jnp.sum(jnp.where(ii < jj, jnp.broadcast_to(hit, (nr, nr)), 0.0), axis=0, keepdims=True)
            rank_row = jnp.where(hit_row > 0, rank_row, -1.0)
            rank = jnp.where(hit > 0, rank, -1.0)
            want = jnp.sum(jnp.where(rank_row == col_rank, col_value, 0.0), axis=1, keepdims=True) - 1.0
            want_row = jnp.sum(jnp.where(rank == row_rank, row_value, 0.0), axis=0, keepdims=True) - 1.0
            sel[s, b * SLOTS : (b + 1) * SLOTS, :] = jnp.where(want == lane_row, 1.0, 0.0).astype(BF)

            def chip(c):
                here = pl.ds(pl.multiple_of(c * chunk, TILE), chunk)
                selt[s, here, b * SLOTS : (b + 1) * SLOTS] = jnp.where(
                    chip_row == want_row - (c * real).astype(F32), 1.0, 0.0
                ).astype(BF)

            loop(2 * ny, chip)

    def outputs():
        yc[...] = xy_arrive(1)

    own = place(core, 0)
    x_copies = gather_copies(xg, 0)
    xg[own, :] = xy_arrive(0)
    loop(tiles, functools.partial(gather_start, x_copies))

    def turn(src, out, lo, hi):
        def one(n):
            here = pl.ds(pl.multiple_of((n + lo) * LANE, LANE), LANE)
            out[here, :] = src[:, here].T

        loop(hi - lo, one)

    def turn_part(src, out, i):
        count = src.shape[1] // LANE
        turn(src, out, count * i // stages, count * (i + 1) // stages)

    def choose_part(i):
        lo, hi = layers * i // stages, layers * (i + 1) // stages
        loop(hi - lo, lambda s: choose(s + lo))

    gather_run(x_copies, [functools.partial(choose_part, i) for i in range(stages)])
    outputs()
    for copy in enc_loads:
        copy.wait()

    def lat_rows(j):
        return pl.ds(pl.multiple_of(j * shard, 16), shard)

    nz = nl // 2

    def peer_of(d):
        j = (d - 1) // 2
        away = nz // 2 + (j + 1) // 2 * (1 - 2 * lax.rem(j, 2))
        there = lax.rem(q // nz + d, 2)
        return there * nz + lax.rem(lax.rem(q, nz) + away, nz)

    def scatter(src, dst, s, n):
        def one(d, carry):
            peer = peer_of(d)
            pltpu.make_async_remote_copy(
                src.at[s, lat_rows(peer)], dst.at[s, q], lat_s.at[n, s], lat_r.at[n, s],
                device_id={"layer": me, "lat": peer},
            ).start()
            return carry

        lax.fori_loop(1, nl, one, 0)
        dst[s, q] = src[s, lat_rows(q), :]

    def spread(buf, s, n):
        def one(d, carry):
            where = buf.at[s, lat_rows(q)]
            pltpu.make_async_remote_copy(
                where, where, lat_s.at[n, s], lat_r.at[n, s], device_id={"layer": me, "lat": peer_of(d)}
            ).start()
            return carry

        lax.fori_loop(1, nl, one, 0)

    def lat_wait(sem, s, n):
        where = ck.at[s, pl.ds(0, (nl - 1) * shard)]
        pltpu.make_async_copy(where, where, sem.at[n, s]).wait()

    def pack(dense, dst, s):
        both = dot(sel[s], dense)
        for b in range(2):
            part = slice(b * SLOTS, (b + 1) * SLOTS)
            dst[s, part, :] = both[part, b * BLOCK : (b + 1) * BLOCK].astype(BF)

    def lane_block(s):
        return pl.ds(pl.multiple_of(s * lats, LANE), lats)

    def encode(s):
        start = jnp.minimum(dl * s // LANE * LANE, width - span)
        dense = dot(xg[:, pl.ds(pl.multiple_of(start, LANE), span)], encp[s]).astype(BF)
        pack(dense, pk, s)
        scatter(pk, rx, s, 0)

    loop(layers, encode)
    for copy in dec_loads:
        copy.wait()
    turn(dcat, dturn, 0, layers * lats // LANE)

    b_of = q * shard // SLOTS
    def activate(s):
        lat_wait(lat_r, s, 0)
        total = jnp.sum(rx[s].astype(F32), axis=0)
        bias = bias_in[pl.ds(s, 1), :]
        pre = total + jnp.where(b_of == 0, bias[:, 0:BLOCK], bias[:, BLOCK : 2 * BLOCK])
        small = jnp.exp(-jnp.abs(pre))
        ck[s, lat_rows(q), :] = (jnp.maximum(pre, 0.0) + jnp.log1p(small)).astype(BF)
        slope[s] = jnp.where(pre >= 0, 1.0, small) / (1.0 + small)
        spread(ck, s, 1)

    loop(layers, activate)

    def unpack(src, dst, s):
        zero = jnp.zeros((SLOTS, BLOCK), BF)
        wide = jnp.concatenate(
            [
                jnp.concatenate([src[s, 0:SLOTS, :], zero], axis=1),
                jnp.concatenate([zero, src[s, SLOTS : 2 * SLOTS, :]], axis=1),
            ],
            axis=0,
        )
        dst[:, lane_block(s)] = dot(selt[s], wide).astype(BF)

    def codes(s):
        lat_wait(lat_r, s, 1)
        unpack(ck, cd, s)

    loop(layers, codes)

    groups = []
    for n in range(width // LANE):
        count = min(layers, ((n + 1) * LANE - 1) // dl + 1)
        if groups and groups[-1][2] == count:
            groups[-1][1] = n + 1
        else:
            groups.append([n, n + 1, count])

    uses = [na, na - 1, -nb]
    for i in range(1, nb):
        uses += [na - 1 - i, i - nb]
    uses.append(0)

    def hm_copy(offset, sign):
        where = place(0, sign * offset)
        return pltpu.make_async_remote_copy(
            hm_s.at[where], hm_r.at[where], hm_out.at[0], hm_sem.at[uses.index(offset)], device_id=mate
        )

    def decode(j):
        hh = jnp.where(j == 0, 1 - core, core)
        base = pl.ds(pl.multiple_of(hh * half, TILE), half)
        for lo, hi, count in groups:
            lanes = slice(lo * LANE, hi * LANE)
            ho[:, lanes] = dot(cd[base, 0 : count * lats], dturn[0 : count * lats, lanes])

        @pl.when(j == 0)
        def _():
            hm_s[...] = ho[...].astype(BF)
            for offset in uses:
                hm_copy(offset, -1).start()

    loop(2, decode)

    def mine(offset, c):
        where = tile_of(0, offset, c)
        return ho[where, :] + hm_r[where, :].astype(F32)

    def small_tile(c):
        return pl.ds(pl.multiple_of(c * TILE, TILE), TILE)

    def a_copy(i, c):
        return pltpu.make_async_remote_copy(
            ra_s.at[i, small_tile(c)],
            ra_r.at[i, small_tile(c)],
            rs_out.at[0],
            rs_ar.at[i, c],
            device_id=to_a if i else two_a,
        )

    def b_copy(i, c):
        return pltpu.make_async_remote_copy(
            rb_s.at[i, small_tile(c)], rb_r.at[i, small_tile(c)], rs_out.at[0], rs_br.at[i, c], device_id=to_b
        )

    def forward(copy, buf_s, buf_r, i, offset, earlier, c):
        part = mine(offset, c)
        for n in earlier:
            copy(n, c).wait_recv()
            part = part + buf_r[n, small_tile(c), :].astype(F32)
        buf_s[i, small_tile(c), :] = part.astype(BF)
        copy(i, c).start()

    def from_a(i):
        return [] if i < 2 else [0, 1] if i == 2 else [i - 1]

    for i in range(stages):
        now = [na, na - 1, -nb] if i == 0 else [na - 1 - i, i - nb]
        for offset in now:
            hm_copy(offset, 1).wait_recv()

        def both(c):
            if i == 0:
                forward(a_copy, ra_s, ra_r, 0, na, [], c)
            forward(a_copy, ra_s, ra_r, i + 1, na - 1 - i, from_a(i + 1), c)
            forward(b_copy, rb_s, rb_r, i, i - nb, [i - 1] if i else [], c)

        loop(tiles, both)
        turn_part(xg, xt, i)

    hm_copy(0, 1).wait_recv()

    def fx_copy(c):
        here = small_tile(c)
        return pltpu.make_async_remote_copy(
            fx_s.at[here], fx_r.at[here], fx_out.at[0], fx_sem.at[c], device_id=partner
        )

    def finish(c):
        here = small_tile(c)
        total = mine(0, c)
        for n in from_a(na):
            a_copy(n, c).wait_recv()
            total = total + ra_r[n, here, :].astype(F32)
        b_copy(nb - 1, c).wait_recv()
        total = total + rb_r[nb - 1, here, :].astype(F32)
        fx_s[here, :] = total.astype(BF)
        fx_copy(c).start()

    loop(tiles, finish)

    e_copies = gather_copies(eg, 1)

    def differ(c):
        here = small_tile(c)
        fx_copy(c).wait_recv()
        whole = fx_s[here, :].astype(F32) + fx_r[here, :].astype(F32)
        eg[tile_of(core, 0, c), :] = (whole - yc[here, :].astype(F32)).astype(BF)
        gather_start(e_copies, c)
        ho[here, :] = whole

    loop(tiles, differ)

    @pl.when(owner)
    def _():
        recb[...] = ho[0:chunk, :].astype(BF)

    rec_copy = pltpu.make_async_remote_copy(recb, recb, rec_sem.at[0], rec_sem.at[1], device_id=mate)

    @pl.when(owner)
    def _():
        rec_copy.start()

    gather_run(e_copies, [])

    def out_copy(buf, ref, n, sem):
        return pltpu.make_async_copy(buf.at[n], ref.at[n], out_sem.at[sem])

    def back(s):
        low = dl * s // LANE * LANE
        dense = dot(eg[:, low:width], dcat[low:width, s * lats : (s + 1) * lats]).astype(BF)
        pack(dense, pc, s)
        scatter(pc, rc, s, 2)

    for s in range(layers - 1, -1, -1):
        back(s)
    turn(eg, et, 0, width // LANE)

    def decoder_grad(pair):
        t = jnp.int32(0)
        for n in range(1, layers):
            t = t + jnp.where(pair >= n * (n + 1) // 2, 1, 0)
        s = pair - t * (t + 1) // 2
        out = dot(et[pl.ds(pl.multiple_of(t * dl, TILE), dl), :], cd[:, lane_block(s)])
        dgb[pair] = out.astype(BF)
        out_copy(dgb, dg_ref, pair, layers + pair).start()

    pairs = dg_ref.shape[0]

    def settle(s):
        lat_wait(lat_r, s, 2)
        total = jnp.sum(rc[s].astype(F32), axis=0)
        pg[s, lat_rows(q), :] = (total * slope[s]).astype(BF)
        spread(pg, s, 3)

    loop(layers, lambda i: settle(layers - 1 - i))
    loop(pairs, decoder_grad)

    @pl.when(owner)
    def _():
        rec_copy.wait_send()

    @pl.when(jnp.logical_not(owner))
    def _():
        rec_copy.wait_recv()

    take = jnp.where(iota((rows, chunk), 1) == iota((rows, chunk), 0) + rows * core, 1.0, 0.0).astype(BF)
    out = dot(take, recb[...]).astype(BF)
    for t in range(layers):
        rec_ref[:, t, :] = out[:, t * dl : (t + 1) * dl]


    def encoder_grad(s):
        lat_wait(lat_r, s, 3)
        unpack(pg, pgd, s)
        for b in range(2):
            bsum[s, :, b * BLOCK : (b + 1) * BLOCK] = jnp.sum(
                pg[s, b * SLOTS : (b + 1) * SLOTS, :].astype(F32), axis=0, keepdims=True
            )
        egb[s] = dot(xt[pl.ds(pl.multiple_of(s * dl, TILE), dl), :], pgd[:, lane_block(s)]).astype(BF)
        out_copy(egb, eg_ref, s, s).start()

    loop(layers, lambda i: encoder_grad(layers - 1 - i))
    for s in range(layers):
        bg_ref[s : s + 1, :] = bsum[s]

    for n in range(2):
        xy_copy(n, mate, core).wait_send()

        @pl.when(jnp.logical_not(owner))
        def _():
            xy_copy(n, mate, 1 - core).wait_send()

    loop(layers, lambda s: out_copy(egb, eg_ref, s, s).wait())
    loop(pairs, lambda n: out_copy(dgb, dg_ref, n, layers + n).wait())
    sent(hm_s, half, hm_out.at[0])
    sent(xg, chunk, fx_out.at[0])
    sent(xg, (na + nb) * chunk, rs_out.at[0])
    for n in range(2):
        sent(xg, (na + nb + ny) * chunk, ag_out.at[n])
    for n in range(4):
        for s in range(layers):
            lat_wait(lat_s, s, n)


def hand_over(*refs):
    count = (len(refs) - 2) // 3
    come, go = refs[-2:]
    copies = []
    for n in range(count):
        src, dst, mid = refs[n], refs[count + n], refs[2 * count + n]
        parts = src.shape[0] if n in (1, 3) else 1
        for p in range(parts):
            a, b, c = (src.at[p], mid.at[p], dst.at[p]) if parts > 1 else (src, mid, dst)
            k = len(copies)
            copies.append((pltpu.make_async_copy(a, b, come.at[k]), pltpu.make_async_copy(b, c, go.at[k])))
    for first, _ in copies:
        first.start()
    for first, second in copies:
        first.wait()
        second.start()
    for _, second in copies:
        second.wait()


def step(sizes, layer_inputs, layer_outputs, encoder, encoder_bias, decoder, active_blocks):
    layers, dl, lats, rows, ny, nl, chunk = sizes
    width = layers * dl
    places = 2 * ny * chunk
    na, nb = ny // 2, max(1, ny // 2 - 1)
    shard = 2 * SLOTS // nl
    pairs = decoder.shape[0]
    vmem, dma = pltpu.VMEM, pltpu.SemaphoreType.DMA
    ring, tiles = (chunk, width), chunk // TILE
    scratch = [
        vmem((places, width), BF),
        vmem((places, width), BF),
        vmem((width, places), BF),
        vmem((width, places), BF),
        vmem((places, layers * lats), BF),
        vmem((places, layers * lats), BF),
        vmem((layers, 3 * LANE, lats), BF),
        vmem((width, layers * lats), BF),
        vmem((layers * lats, width), BF),
        vmem((layers, 2 * SLOTS, places), BF),
        vmem((layers, places, 2 * SLOTS), BF),
        vmem((2, 32, width), BF),
        vmem((2, 2, 32, width), BF),
        vmem((layers, 2 * SLOTS, BLOCK), BF),
        vmem((layers, nl, shard, BLOCK), BF),
        vmem((layers, 2 * SLOTS, BLOCK), BF),
        vmem((layers, 2 * SLOTS, BLOCK), BF),
        vmem((layers, nl, shard, BLOCK), BF),
        vmem((layers, 2 * SLOTS, BLOCK), BF),
        vmem((layers, shard, BLOCK), F32),
        vmem((places // 2, width), BF),
        vmem((places // 2, width), BF),
        vmem((places // 2, width), F32),
        vmem((na,) + ring, BF),
        vmem((na,) + ring, BF),
        vmem((nb,) + ring, BF),
        vmem((nb,) + ring, BF),
        vmem(ring, BF),
        vmem(ring, BF),
        vmem(ring, BF),
        vmem(ring, BF),
        vmem((rows, layers, dl), BF),
        vmem((rows, layers, dl), BF),
        vmem((layers, active_blocks.shape[2], active_blocks.shape[1]), jnp.int32),
        vmem((layers, lats), F32),
        vmem((layers, 1, lats), F32),
        vmem((layers, dl, lats), BF),
        vmem((pairs, dl, lats), BF),
        dma((4 + layers + pairs,)),
        dma((2, 2)),
        dma((2, 2)),
        dma((2,)),
        dma((2, na, tiles)),
        dma((2, nb, tiles)),
        dma((2, ny)),
        dma((4, layers)),
        dma((4, layers)),
        dma((1,)),
        dma((ny,)),
        dma((1,)),
        dma((na, tiles)),
        dma((nb, tiles)),
        dma((1,)),
        dma((tiles,)),
        dma((2,)),
        dma((layers + pairs,)),
    ]
    in_vmem = pl.BlockSpec(memory_space=pltpu.VMEM)
    hbm = pl.BlockSpec(memory_space=pltpu.HBM)
    made = pl.pallas_call(
        functools.partial(kernel, sizes),
        out_shape=(
            jax.ShapeDtypeStruct((rows, layers, dl), BF),
            jax.ShapeDtypeStruct((layers, dl, lats), BF),
            jax.ShapeDtypeStruct((layers, lats), F32),
            jax.ShapeDtypeStruct((pairs, dl, lats), BF),
        ),
        in_specs=[hbm] * 6,
        out_specs=(in_vmem, hbm, in_vmem, hbm),
        scratch_shapes=scratch,
        compiler_params=pltpu.CompilerParams(
            collective_id=0, has_side_effects=True, vmem_limit_bytes=56 * 1024 * 1024
        ),
    )(
        layer_inputs.transpose(2, 0, 1),
        layer_outputs,
        encoder,
        encoder_bias,
        decoder,
        active_blocks.transpose(0, 2, 1),
    )
    return pl.pallas_call(
        hand_over,
        out_shape=tuple(jax.ShapeDtypeStruct(v.shape, v.dtype) for v in made),
        in_specs=[hbm] * 4,
        out_specs=(hbm,) * 4,
        scratch_shapes=[vmem(v.shape, v.dtype) for v in made] + [dma((layers + pairs + 2,))] * 2,
        compiler_params=pltpu.CompilerParams(vmem_limit_bytes=56 * 1024 * 1024),
    )(*made)


def solution(mesh):
    ny, nl = mesh.shape["layer"] // 4, mesh.shape["lat"]

    def local(layer_inputs, layer_outputs, encoder, encoder_bias, decoder, active_blocks):
        layers, dl, lats = encoder.shape
        rows = layer_outputs.shape[0]
        chunk = -(-2 * rows // 16) * 16
        sizes = (layers, dl, lats, rows, ny, nl, chunk)
        return step(sizes, layer_inputs, layer_outputs, encoder, encoder_bias, decoder, active_blocks)

    return jax.shard_map(
        local,
        mesh=mesh,
        in_specs=(
            P(None, "lat", "layer"),
            P("layer", None, "lat"),
            P(None, "lat", "layer"),
            P(None, "layer"),
            P(None, "lat", "layer"),
            P(),
        ),
        out_specs=(
            P("layer", None, "lat"),
            P(None, "lat", "layer"),
            P(None, "layer"),
            P(None, "lat", "layer"),
        ),
        check_vma=False,
    )
```
